256 devices in a mesh: brick: 32 (over x, z), region: 8 (over y, core).
Axes of the slice: x: 4, y: 4, z: 8, core: 2. Of those that a mesh axis runs over, the one named last changes fastest.
Arguments:
- segments: float32 [8192, 8, 128], P(('brick', 'region'))
- ship_list: int32 [256, 32, 4], P(('brick', 'region')), may hold values from 0 to 31
- kept_tiles: int32 [256, 64, 2], P(('brick', 'region')), may hold values from 0 to 159
- kept_count: int32 [256], P(('brick', 'region')), may hold values from 1 to 64, as said below
- lent_tiles: int32 [256, 8, 8, 2], P(('brick', 'region')), may hold values from 0 to 159
- lent_count: int32 [32, 8, 8], P('brick'), may hold values from 0 to 8, as said below
Outputs:
- loads: float32 [8192, 6, 128], P(('brick', 'region'))
The draws below stay inside these ranges and needn't reach their ends.
Inputs may be any that keep to these rules, and one draw needn't show every extreme that they name: `kept_count`: in every brick one device has exactly 64 live kept slots. `lent_count`: zero where i equals j; in every brick some entry equals 8.
All inputs are finite; a program needn't handle non-finite values.
Results may differ from the reference program's by a relative error of at most 0.0001.
Values sent between devices are 32-bit elements; how exact they have to be, the bound alone decides.
A program may use at most 64 MiB of HBM per device.

```python
import jax
import jax.numpy as jnp
from jax import lax

SEG = 128
LEAVES_DEV = 32
GSLOT = 4
KEEP = 64
LEND = 8
LEAVES = 8192
EXT = 160
N_BRICK = 32
N_REGION = 8
DEVICES = 256


def heavy_devices(key):
    return jax.random.randint(jax.random.fold_in(key, 11), (N_BRICK,), 0, N_REGION)


def draw_segments(key, part):
    keys = jax.random.split(key, 6)
    shape = (LEAVES, SEG)
    start = jax.random.uniform(keys[0], (LEAVES, 3, SEG), jnp.float32, 0.0, 1.2)
    modulus = jnp.exp(jax.random.uniform(keys[5], shape, jnp.float32, 0.0, jnp.log(10.0)))
    sign = jnp.where(jax.random.uniform(keys[1], shape, jnp.float32) < 0.5, 1.0, -1.0)
    along = sign * jax.random.uniform(keys[2], shape, jnp.float32, 0.25, 0.5)
    across = jax.random.uniform(keys[3], (LEAVES, 2, SEG), jnp.float32, -0.3, 0.3)
    radius = jax.random.uniform(keys[4], shape, jnp.float32, 0.06, 0.14)
    rows = [start, along[:, None, :], across, radius[:, None, :], modulus[:, None, :]]
    return jnp.concatenate(rows, axis=1).astype(jnp.float32)


def draw_kept_count(key, part):
    heavy = heavy_devices(key)
    counts = jax.random.randint(jax.random.fold_in(key, 12), (DEVICES,), 1, KEEP // 2 + 1)
    devices = jnp.arange(DEVICES)
    return jnp.where(devices % N_REGION == heavy[devices // N_REGION], KEEP, counts).astype(jnp.int32)


def draw_lent_count(key, part):
    heavy = heavy_devices(key)
    counts = jax.random.randint(jax.random.fold_in(key, 13), (N_BRICK, N_REGION, N_REGION), 0, LEND + 1)
    source = jnp.arange(N_REGION)[None, :, None]
    target = jnp.arange(N_REGION)[None, None, :]
    counts = jnp.where(source == target, 0, counts)
    chosen = (source == heavy[:, None, None]) & (target == (heavy[:, None, None] + 1) % N_REGION)
    return jnp.where(chosen, LEND, counts).astype(jnp.int32)


def plant(entries, stream_key, smallest, top_value):
    place = [jax.random.randint(jax.random.fold_in(stream_key, axis), (), 0, length) for axis, length in enumerate(entries.shape)]
    widest = entries.shape.index(max(entries.shape))
    next_to = place[:widest] + [(place[widest] + 1) % entries.shape[widest]] + place[widest + 1:]
    return entries.at[tuple(place)].set(smallest).at[tuple(next_to)].set(top_value)


def setup_inputs(seed: int = 0) -> dict:
    key_list = jax.random.split(jax.random.key(seed), 7)
    segments = draw_segments(jax.random.fold_in(key_list[6], 71), 0)
    ship_list = plant(jax.random.randint(key_list[1], (DEVICES, N_BRICK, GSLOT), 0, LEAVES_DEV), jax.random.fold_in(key_list[1], 1), 0, LEAVES_DEV - 1).astype(jnp.int32)
    kept_tiles = plant(jax.random.randint(key_list[2], (DEVICES, KEEP, 2), 0, EXT), jax.random.fold_in(key_list[2], 1), 0, EXT - 1).astype(jnp.int32)
    kept_count = draw_kept_count(jax.random.fold_in(key_list[6], 71), 0)
    lent_tiles = plant(jax.random.randint(key_list[4], (DEVICES, N_REGION, LEND, 2), 0, EXT), jax.random.fold_in(key_list[4], 1), 0, EXT - 1).astype(jnp.int32)
    lent_count = draw_lent_count(jax.random.fold_in(key_list[6], 71), 0)
    return dict(segments=segments, ship_list=ship_list, kept_tiles=kept_tiles, kept_count=kept_count, lent_tiles=lent_tiles, lent_count=lent_count)


DIST_FLOOR = 0.0025
PARALLEL_FLOOR = 0.05
REF_GROUP = 64

def cross_rows(lever, force):
    return jnp.stack([lever[:, 1] * force[:, 2] - lever[:, 2] * force[:, 1], lever[:, 2] * force[:, 0] - lever[:, 0] * force[:, 2], lever[:, 0] * force[:, 1] - lever[:, 1] * force[:, 0]], axis=1)

def pair_forces(left, right):
    start_a = left[:, 0:3, :, None]
    axis_a = left[:, 3:6, :, None]
    radius_a = left[:, 6, :, None]
    modulus_a = left[:, 7, :, None]
    start_b = right[:, 0:3, None, :]
    axis_b = right[:, 3:6, None, :]
    radius_b = right[:, 6, None, :]
    modulus_b = right[:, 7, None, :]
    offset = start_a - start_b
    len_a = lax.optimization_barrier(jnp.sum(axis_a * axis_a, axis=1))
    len_b = lax.optimization_barrier(jnp.sum(axis_b * axis_b, axis=1))
    cosine = lax.optimization_barrier(jnp.sum(axis_a * axis_b, axis=1))
    proj_a = lax.optimization_barrier(jnp.sum(axis_a * offset, axis=1))
    proj_b = lax.optimization_barrier(jnp.sum(axis_b * offset, axis=1))
    denom = jnp.maximum(len_a * len_b - cosine * cosine, PARALLEL_FLOOR * len_a * len_b)
    param_a = jnp.clip((cosine * proj_b - proj_a * len_b) / denom, 0.0, 1.0)
    param_b = jnp.clip((cosine * param_a + proj_b) / len_b, 0.0, 1.0)
    param_a = jnp.clip((cosine * param_b - proj_a) / len_a, 0.0, 1.0)
    gap = offset + param_a[:, None] * axis_a - param_b[:, None] * axis_b
    dist = jnp.sqrt(jnp.maximum(lax.optimization_barrier(jnp.sum(gap * gap, axis=1)), DIST_FLOOR))
    depth = jnp.maximum(radius_a + radius_b - dist, 0.0)
    stiff = 4.0 / 3.0 * modulus_a * modulus_b / (modulus_a + modulus_b) * jnp.sqrt(radius_a * radius_b / (radius_a + radius_b))
    scale = stiff * depth * jnp.sqrt(depth) / dist
    force = scale[:, None] * gap
    torque_a = cross_rows((param_a - 0.5)[:, None] * axis_a, force)
    torque_b = cross_rows((param_b - 0.5)[:, None] * axis_b, -force)
    on_a = jnp.concatenate([lax.optimization_barrier(jnp.sum(force, axis=3)), lax.optimization_barrier(jnp.sum(torque_a, axis=3))], axis=1)
    on_b = jnp.concatenate([-lax.optimization_barrier(jnp.sum(force, axis=2)), lax.optimization_barrier(jnp.sum(torque_b, axis=2))], axis=1)
    return (on_a, on_b)

def reference(segments, ship_list, kept_tiles, kept_count, lent_tiles, lent_count):
    devices = jnp.arange(DEVICES).astype(jnp.int32)

    def to_global(ext, owner):
        ghost = jnp.maximum(ext - LEAVES_DEV, 0)
        source = ghost // GSLOT * N_REGION + owner % N_REGION
        leaf = ship_list[source, owner // N_REGION, ghost % GSLOT]
        return jnp.where(ext < LEAVES_DEV, owner * LEAVES_DEV + ext, source * LEAVES_DEV + leaf).astype(jnp.int32)
    kept_owner = devices[:, None]
    kept_a = to_global(kept_tiles[:, :, 0], kept_owner)
    kept_b = to_global(kept_tiles[:, :, 1], kept_owner)
    kept_live = jnp.arange(KEEP).astype(jnp.int32)[None, :] < kept_count[:, None]
    lent_owner = devices[:, None, None]
    lent_a = to_global(lent_tiles[..., 0], lent_owner)
    lent_b = to_global(lent_tiles[..., 1], lent_owner)
    plan = lent_count[devices // N_REGION, devices % N_REGION]
    lent_live = jnp.arange(LEND).astype(jnp.int32)[None, None, :] < plan[:, :, None]
    first = jnp.concatenate([kept_a.reshape(-1), lent_a.reshape(-1)])
    second = jnp.concatenate([kept_b.reshape(-1), lent_b.reshape(-1)])
    live = jnp.concatenate([kept_live.reshape(-1), lent_live.reshape(-1)])
    extra = -first.shape[0] % REF_GROUP
    first = jnp.pad(first, (0, extra)).reshape(-1, REF_GROUP)
    second = jnp.pad(second, (0, extra)).reshape(-1, REF_GROUP)
    live = jnp.pad(live, (0, extra)).reshape(-1, REF_GROUP)

    def group_step(acc, item):
        group_a, group_b, group_live = item
        on_a, on_b = pair_forces(segments[group_a], segments[group_b])
        keep = group_live[:, None, None]
        acc = acc.at[group_a].add(jnp.where(keep, on_a, 0.0))
        acc = acc.at[group_b].add(jnp.where(keep, on_b, 0.0))
        return (acc, None)
    zeros = jnp.zeros((LEAVES, 6, SEG), jnp.float32)
    loads, _ = lax.scan(group_step, zeros, (first, second, live))
    return loads
```

```python
import functools
import jax, jax.numpy as jnp
from jax import lax
from jax.experimental import pallas as pl
from jax.experimental.pallas import tpu as pltpu
from jax.sharding import PartitionSpec as P

MESH = pl.DeviceIdType.MESH
F32, BF16 = jnp.float32, jnp.bfloat16
DIST_FLOOR = 0.0025
PARALLEL_FLOOR = 0.05
TINY = 1e-20
DEPTH = 80

def split3(x):
    hi = x.astype(BF16).astype(F32)
    rest = x - hi
    mid = rest.astype(BF16).astype(F32)
    return hi, mid, rest - mid

def rowsum(x, first, last):
    row = lax.broadcasted_iota(jnp.int32, x.shape, 0)
    return jnp.sum(jnp.where((row >= first) & (row < last), x, 0.0), axis=0, keepdims=True)

def prepare(seg, origin, feat, left, right, blk):
    p = seg[0:3] - origin
    d = seg[3:6]
    a = jnp.sum(d * d, axis=0, keepdims=True)
    inv = lax.rsqrt(a)
    u = d * inv
    length = a * inv
    along = jnp.sum(u * p, axis=0, keepdims=True)
    r = seg[6:7]
    ir = 1.0 / r
    ie = 0.75 / seg[7:8]
    one = jnp.ones_like(r)
    x1 = jnp.concatenate([u, p, along, one], axis=0)
    x2 = jnp.concatenate([length, r, ir, ie, jnp.zeros((4, 128), F32)], axis=0)
    feat[blk, 0:8, :] = x1
    feat[blk, 8:16, :] = x2
    h1, m1, l1 = split3(x1)
    h2, m2, l2 = split3(x2)
    rows = jnp.concatenate([h1, h1, m1, m1, h1, l1, h2, m2, l2, jnp.zeros((128 - 72, 128), F32)], axis=0)
    left[blk] = rows.T.astype(BF16)
    z = jnp.zeros((3, 128), F32)
    z1 = jnp.zeros((1, 128), F32)
    for q, part in enumerate((
        jnp.concatenate([u, z, z1, z1], axis=0),
        jnp.concatenate([-p, z, one, z1], axis=0),
        jnp.concatenate([z, u, z1, -along], axis=0),
    )):
        h, m, l = split3(part)
        right[blk, :, 128 * q:128 * q + 128] = jnp.concatenate([h, m, h, m, l, h], axis=0).astype(BF16)

def spread_matrix():
    row = lax.broadcasted_iota(jnp.int32, (128, 128), 0)
    cols = []
    for q in range(6):
        cols.append((row == q) | (row == 16 + q) | (row == 40 + q))
    for q in range(4):
        cols.append((row == 48 + q) | (row == 56 + q) | (row == 64 + q))
    return jnp.concatenate([jnp.where(c, 1.0, 0.0) for c in cols], axis=1).astype(BF16)

def products(a, b, left, right, spread, dots, wide):
    lhs = left[a]
    dots[...] = jnp.dot(lhs[:, 0:48], right[b], preferred_element_type=F32)
    wide[...] = jnp.dot(lhs, spread[...], preferred_element_type=F32)

def tile(b, feat, dots, wide, cols):
    def lane(q):
        return jnp.broadcast_to(feat[b, q:q + 1, :], (8, 128))
    u2 = [lane(q) for q in range(3)]
    p2 = [lane(3 + q) for q in range(3)]
    len2, r2, ir2, ie2 = [lane(8 + q) for q in range(4)]
    fsum = [None] * 6
    for g in range(16):
        rs = slice(8 * g, 8 * g + 8)
        w, c, f = [dots[rs, 128 * q:128 * q + 128] for q in range(3)]
        wd = [wide[rs, 128 * q:128 * q + 128] for q in range(10)]
        u1, p1 = wd[0:3], wd[3:6]
        len1, r1, ir1, ie1 = wd[6:10]
        den = jnp.maximum(1.0 - w * w, PARALLEL_FLOOR)
        s = (w * f - c) * pltpu.reciprocal(den, approx=True)
        s = jnp.minimum(jnp.maximum(s, 0.0), len1)
        t = jnp.minimum(jnp.maximum(w * s + f, 0.0), len2)
        s = jnp.minimum(jnp.maximum(w * t - c, 0.0), len1)
        gap = [(p1[q] - p2[q]) + s * u1[q] - t * u2[q] for q in range(3)]
        m = jnp.maximum(gap[0] * gap[0] + gap[1] * gap[1] + gap[2] * gap[2], DIST_FLOOR)
        y = lax.rsqrt(m)
        h = jnp.maximum(r1 + r2 - m * y, TINY)
        k = (h * h) * (lax.rsqrt(h * (ir1 + ir2)) * y) * pltpu.reciprocal(ie1 + ie2, approx=True)
        force = [k * x for x in gap]
        vals = force + [s * x for x in force]
        for q in range(6):
            cols[rs, q:q + 1] = jnp.sum(vals[q], axis=1, keepdims=True)
        back = force + [t * x for x in force]
        for q in range(6):
            fsum[q] = back[q] if g == 0 else fsum[q] + back[q]
    on_a = cols[...].T[0:8]
    on_b = -jnp.concatenate([jnp.sum(x, axis=0, keepdims=True) for x in fsum], axis=0)
    return on_a, on_b


def greet(bricks):
    me = lax.axis_index("brick")
    barrier = pltpu.get_barrier_semaphore()
    for off in range(1, bricks):
        pl.semaphore_signal(barrier, inc=1, device_id={"brick": lax.rem(me + off, bricks)}, device_id_type=MESH)
    return me, barrier

def send_kernel(bricks, slots, seg, ship, ext, stage, send_sem, recv_sem):
    me, barrier = greet(bricks)
    leaves = seg.shape[0]
    ext[0:leaves] = seg[...]
    for q in range(bricks):
        for k in range(slots):
            stage[q * slots + k] = seg[ship[q * slots + k]]
    pl.semaphore_wait(barrier, bricks - 1)
    mine = ext.at[pl.ds(leaves + me * slots, slots)]
    for off in range(1, bricks):
        q = lax.rem(me + off, bricks)
        pltpu.make_async_remote_copy(
            src_ref=stage.at[pl.ds(q * slots, slots)], dst_ref=mine, send_sem=send_sem, recv_sem=recv_sem,
            device_id={"brick": q}, device_id_type=MESH).start()
    ext[pl.ds(leaves + me * slots, slots)] = stage[pl.ds(me * slots, slots)]
    total = (bricks - 1) * slots
    pltpu.make_async_copy(stage.at[0:total], ext.at[0:total], recv_sem).wait()
    pltpu.make_async_copy(stage.at[0:total], ext.at[0:total], send_sem).wait()

def back_kernel(bricks, slots, ghosts, back, send_sem, recv_sem):
    me, barrier = greet(bricks)
    pl.semaphore_wait(barrier, bricks - 1)
    rows = 6 * slots
    for off in range(1, bricks):
        q = lax.rem(me + off, bricks)
        pltpu.make_async_remote_copy(
            src_ref=ghosts.at[q], dst_ref=back.at[me], send_sem=send_sem, recv_sem=recv_sem,
            device_id={"brick": q}, device_id_type=MESH).start()
    back[me] = ghosts[me]
    pltpu.make_async_copy(ghosts.at[0:bricks - 1], back.at[0:bricks - 1], recv_sem).wait()
    pltpu.make_async_copy(ghosts.at[0:bricks - 1], back.at[0:bricks - 1], send_sem).wait()

def tile_kernel(leaves, seg, kept, kept_count, lent, plan, own, ghosts, ids_a, ids_b, acc, feat, left, right, spread,
                dots0, dots1, wide0, wide1, cols0, cols1):
    blocks = seg.shape[0]
    region = lax.axis_index("region")
    origin = jnp.broadcast_to(seg[0, 0:3, 0:1], (3, 128))
    spread[...] = spread_matrix()
    acc[...] = jnp.zeros_like(acc)
    cols0[...] = jnp.zeros_like(cols0)
    cols1[...] = jnp.zeros_like(cols1)
    UN = 4
    def prep(i, _):
        for k in range(UN):
            prepare(seg[i * UN + k], origin, feat, left, right, i * UN + k)
        return 0
    lax.fori_loop(0, blocks // UN, prep, 0)

    n_kept = kept_count[0]
    def list_kept(i, _):
        ids_a[i] = kept[2 * i]
        ids_b[i] = kept[2 * i + 1]
        return 0
    lax.fori_loop(0, n_kept, list_kept, 0)
    regions = plan.shape[1]
    lend = lent.shape[0] // (2 * regions)
    n = n_kept
    for j in range(regions):
        live = plan[region, j]
        def list_lent(i, n, j=j):
            ids_a[n + i] = lent[2 * (j * lend + i)]
            ids_b[n + i] = lent[2 * (j * lend + i) + 1]
            return n
        lax.fori_loop(0, live, list_lent, n)
        n = n + live

    last = n - 1
    def at(t):
        t = jnp.minimum(t, last)
        return ids_a[t], ids_b[t]
    a, b = at(0)
    products(a, b, left, right, spread, dots0, wide0)
    def step(i, _):
        a0, b0 = at(2 * i)
        a1, b1 = at(2 * i + 1)
        products(a1, b1, left, right, spread, dots1, wide1)
        x, y = tile(b0, feat, dots0, wide0, cols0)
        acc[a0, 0:6] += x[0:6]
        acc[b0, 0:6] += y
        a2, b2 = at(2 * i + 2)
        products(a2, b2, left, right, spread, dots0, wide0)
        x, y = tile(b1, feat, dots1, wide1, cols1)
        live = 2 * i + 1 < n
        acc[a1, 0:6] += jnp.where(live, x[0:6], 0.0)
        acc[b1, 0:6] += jnp.where(live, y, 0.0)
        return 0
    lax.fori_loop(0, (n + 1) // 2, step, 0)
    own[...] = acc[0:leaves]
    bricks, rows, _ = ghosts.shape
    slots = rows // 6
    for q in range(bricks):
        for k in range(slots):
            ghosts[q, 6 * k:6 * k + 6] = acc[leaves + q * slots + k, 0:6]

def finish_kernel(slots, seg, ship, own, back, out, acc0, acc1, acc2, acc3):
    accs = (acc0, acc1, acc2, acc3)
    acc0[...] = own[...]
    for acc in accs[1:]:
        acc[...] = jnp.zeros_like(acc)
    bricks = back.shape[0]
    for q in range(bricks):
        for k in range(slots):
            acc = accs[k % 4]
            leaf = ship[q * slots + k]
            acc[leaf, 0:6] += back[q, 6 * k:6 * k + 6]
    for i in range(seg.shape[0]):
        total = acc0[i] + acc1[i] + acc2[i] + acc3[i]
        d = [seg[i, 3 + q:4 + q] for q in range(3)]
        a = d[0] * d[0] + d[1] * d[1] + d[2] * d[2]
        inv = lax.rsqrt(a)
        half = 0.5 * (a * inv)
        u = [x * inv for x in d]
        force = [total[q:q + 1] for q in range(3)]
        lever = [total[3 + q:4 + q] - half * force[q] for q in range(3)]
        torque = [u[(q + 1) % 3] * lever[(q + 2) % 3] - u[(q + 2) % 3] * lever[(q + 1) % 3] for q in range(3)]
        out[i] = jnp.concatenate(force + torque, axis=0)

VM = pl.BlockSpec(memory_space=pltpu.VMEM)
SM = pl.BlockSpec(memory_space=pltpu.SMEM)

def body(segments, ship_list, kept_tiles, kept_count, lent_tiles, lent_count):
    leaves, _, width = segments.shape
    bricks = lax.axis_size("brick")
    slots = ship_list.shape[2]
    ghosts = bricks * slots
    blocks = leaves + ghosts
    shape = lambda *s: jax.ShapeDtypeStruct(s, F32)
    ship = ship_list.reshape(-1)
    kept = kept_tiles.reshape(-1)
    lent = lent_tiles.reshape(-1)
    limit = 48 * 2**20
    ext = pl.pallas_call(
        functools.partial(send_kernel, bricks, slots),
        out_shape=shape(blocks, 8, width),
        in_specs=[VM, SM], out_specs=VM,
        scratch_shapes=[pltpu.VMEM((ghosts, 8, width), F32), pltpu.SemaphoreType.DMA, pltpu.SemaphoreType.DMA],
        compiler_params=pltpu.CompilerParams(collective_id=0, has_side_effects=True, vmem_limit_bytes=limit),
    )(segments, ship)
    slots_total = kept.shape[0] // 2 + lent.shape[0] // 2
    own, part = pl.pallas_call(
        functools.partial(tile_kernel, leaves),
        out_shape=(shape(leaves, 8, width), shape(bricks, 6 * slots, width)),
        in_specs=[VM, SM, SM, SM, SM], out_specs=(VM, VM),
        scratch_shapes=[
            pltpu.SMEM((slots_total,), jnp.int32), pltpu.SMEM((slots_total,), jnp.int32),
            pltpu.VMEM((blocks, 8, 128), F32),
            pltpu.VMEM((blocks, 16, 128), F32),
            pltpu.VMEM((blocks, 128, 128), BF16),
            pltpu.VMEM((blocks, 48, 384), BF16),
            pltpu.VMEM((128, 1280), BF16),
            pltpu.VMEM((128, 384), F32), pltpu.VMEM((128, 384), F32),
            pltpu.VMEM((128, 1280), F32), pltpu.VMEM((128, 1280), F32),
            pltpu.VMEM((128, 128), F32), pltpu.VMEM((128, 128), F32),
        ],
        compiler_params=pltpu.CompilerParams(vmem_limit_bytes=limit),
    )(ext, kept, kept_count, lent, lent_count[0])
    back = pl.pallas_call(
        functools.partial(back_kernel, bricks, slots),
        out_shape=shape(bricks, 6 * slots, width),
        in_specs=[VM], out_specs=VM,
        scratch_shapes=[pltpu.SemaphoreType.DMA, pltpu.SemaphoreType.DMA],
        compiler_params=pltpu.CompilerParams(collective_id=1, has_side_effects=True, vmem_limit_bytes=limit),
    )(part)
    return pl.pallas_call(
        functools.partial(finish_kernel, slots),
        out_shape=shape(leaves, 6, width),
        in_specs=[VM, SM, VM, VM], out_specs=VM,
        scratch_shapes=[pltpu.VMEM((leaves, 8, width), F32)] * 4,
        compiler_params=pltpu.CompilerParams(vmem_limit_bytes=limit),
    )(segments, ship, own, back)

def solution(mesh):
    placed = (
        P(("brick", "region"), None, None),
        P(("brick", "region"), None, None),
        P(("brick", "region"), None, None),
        P(("brick", "region")),
        P(("brick", "region"), None, None, None),
        P("brick", None, None),
    )
    return jax.shard_map(body, mesh=mesh, in_specs=placed, out_specs=P(("brick", "region"), None, None), check_vma=False)
```

```python
import functools
import jax, jax.numpy as jnp
from jax import lax
from jax.experimental import pallas as pl
from jax.experimental.pallas import tpu as pltpu
from jax.sharding import PartitionSpec as P

MESH = pl.DeviceIdType.MESH
F32, BF16 = jnp.float32, jnp.bfloat16
DIST_FLOOR = 0.0025
PARALLEL_FLOOR = 0.05
TINY = 1e-20
LARGE = 1e30

def split3(x):
    hi = x.astype(BF16).astype(F32)
    rest = x - hi
    mid = rest.astype(BF16).astype(F32)
    return hi, mid, rest - mid

def prepare(seg, origin, feat, left, right, more, blk):
    p = seg[0:3] - origin
    d = seg[3:6]
    a = jnp.sum(d * d, axis=0, keepdims=True)
    inv = lax.rsqrt(a)
    u = d * inv
    length = a * inv
    along = jnp.sum(u * p, axis=0, keepdims=True)
    r = seg[6:7]
    ir = jnp.minimum(1.0 / r, LARGE)
    ie = jnp.minimum(0.75 / seg[7:8], LARGE)
    one = jnp.ones_like(r)
    x1 = jnp.concatenate([u, p, along, one], axis=0)
    x2 = jnp.concatenate([length, r, ir, ie, jnp.zeros((4, 128), F32)], axis=0)
    feat[blk] = jnp.concatenate([u, length, jnp.zeros((4, 128), F32)], axis=0)
    h1, m1, l1 = split3(x1)
    h2, m2, l2 = split3(x2)
    rows = jnp.concatenate([h1, h1, m1, m1, h1, l1, h2, m2, l2, jnp.ones((8, 128), F32), jnp.zeros((128 - 80, 128), F32)], axis=0)
    left[blk] = rows.T.astype(BF16)
    for q, x in enumerate(extra(p, r, ir, ie)):
        more[blk, :, 128 * q:128 * q + 128] = x
    z = jnp.zeros((3, 128), F32)
    z1 = jnp.zeros((1, 128), F32)
    for q, part in enumerate((
        jnp.concatenate([u, z, z1, z1], axis=0),
        jnp.concatenate([-p, z, one, z1], axis=0),
        jnp.concatenate([z, u, z1, -along], axis=0),
    )):
        h, m, l = split3(part)
        right[blk, :, 128 * q:128 * q + 128] = jnp.concatenate([h, m, h, m, l, h], axis=0).astype(BF16)

def extra(p, r, ir, ie):
    row = lax.broadcasted_iota(jnp.int32, (8, 128), 0)
    out = []
    for keep, x in ((-1, -p[0:1]), (-1, -p[1:2]), (-1, -p[2:3]), (1, r), (2, ir), (3, ie)):
        h, m, l = split3(x)
        out.append(jnp.concatenate([jnp.where(row == keep, 1.0, 0.0), h, m, l, jnp.zeros((5, 128), F32)], axis=0).astype(BF16))
    return out

def spread_matrix():
    row = lax.broadcasted_iota(jnp.int32, (128, 128), 0)
    cols = []
    for q in range(6):
        cols.append((row == q) | (row == 16 + q) | (row == 40 + q))
    for q in range(4):
        cols.append((row == 48 + q) | (row == 56 + q) | (row == 64 + q))
    return jnp.concatenate([jnp.where(c, 1.0, 0.0) for c in cols], axis=1).astype(BF16)

def products(a, b, left, right, more, spread, dots, wide):
    lhs = left[a]
    spread[64:80, 384:768] = more[b, :, 0:384]
    spread[64:80, 896:1280] = more[b, :, 384:768]
    dots[...] = jnp.dot(lhs[:, 0:48], right[b], preferred_element_type=F32)
    wide[...] = jnp.dot(lhs[:, 0:80], spread[0:80], preferred_element_type=F32)

def tile(b, feat, dots, wide, diag):
    def lane(q):
        return jnp.broadcast_to(feat[b, q:q + 1, :], (8, 128))
    u2 = [lane(q) for q in range(3)]
    len2 = lane(3)
    fsum = [None] * 6
    asum = [None] * 6
    for g in range(16):
        rs = slice(8 * g, 8 * g + 8)
        w, c, f = [dots[rs, 128 * q:128 * q + 128] for q in range(3)]
        wd = [wide[rs, 128 * q:128 * q + 128] for q in range(10)]
        u1, apart = wd[0:3], wd[3:6]
        len1, reach, ir, ie = wd[6:10]
        den = jnp.maximum(1.0 - w * w, PARALLEL_FLOOR)
        s = (w * f - c) * pltpu.reciprocal(den, approx=True)
        s = jnp.minimum(jnp.maximum(s, 0.0), len1)
        t = jnp.minimum(jnp.maximum(w * s + f, 0.0), len2)
        s = jnp.minimum(jnp.maximum(w * t - c, 0.0), len1)
        gap = [apart[q] + s * u1[q] - t * u2[q] for q in range(3)]
        m = jnp.maximum(gap[0] * gap[0] + gap[1] * gap[1] + gap[2] * gap[2], DIST_FLOOR)
        y = lax.rsqrt(m)
        h = jnp.maximum(reach - m * y, TINY)
        k = (h * h) * (lax.rsqrt(h * ir) * y) * pltpu.reciprocal(ie, approx=True)
        force = [k * x for x in gap]
        vals = force + [s * x for x in force]
        if g < 15:
            for q in range(6):
                red = jnp.sum(vals[q], axis=1, keepdims=True)
                asum[q] = jnp.where(diag == g, red, 0.0 if g == 0 else asum[q])
        back = force + [t * x for x in force]
        for q in range(6):
            fsum[q] = back[q] if g == 0 else fsum[q] + back[q]
    return vals + asum + fsum

def settle(pending, diag, acc, a, b, live):
    vals, asum, fsum = pending[0:6], pending[6:12], pending[12:18]
    for q in range(6):
        red = jnp.sum(vals[q], axis=1, keepdims=True)
        asum[q] = jnp.where(diag == 15, red, asum[q])
    on_a = jnp.concatenate([jnp.sum(x, axis=0, keepdims=True) for x in asum], axis=0)
    on_b = jnp.concatenate([jnp.sum(x, axis=0, keepdims=True) for x in fsum], axis=0)
    acc[a, 0:6] += jnp.where(live, on_a, 0.0)
    acc[b, 0:6] -= jnp.where(live, on_b, 0.0)


def greet(bricks):
    me = lax.axis_index("brick")
    barrier = pltpu.get_barrier_semaphore()
    for off in range(1, bricks):
        pl.semaphore_signal(barrier, inc=1, device_id={"brick": lax.rem(me + off, bricks)}, device_id_type=MESH)
    return me, barrier

WAVES = ((0, 0), (1, 7), (2, 6), (3, 5), (4, 4))
NX, NZ = 4, 8

def wave_offsets(wave):
    first, second = WAVES[wave]
    zs = (first,) if first == second else (first, second)
    return [(dx, dz) for dz in zs for dx in range(NX) if (dx, dz) != (0, 0)]

def send_kernel(bricks, slots, seg, ship, feat, left, right, more, ext, stage, send_sem, recv_sems):
    me, barrier = greet(bricks)
    x, z = me // NZ, lax.rem(me, NZ)
    leaves = seg.shape[0]
    for q in range(bricks):
        for k in range(slots):
            stage[q * slots + k] = seg[ship[k, q]]
    origin = jnp.broadcast_to(seg[0, 0:3, 0:1], (3, 128))
    def own(i, _):
        for k in range(4):
            prepare(seg[4 * i + k], origin, feat, left, right, more, 4 * i + k)
        return 0
    lax.fori_loop(0, leaves // 8, own, 0)
    pl.semaphore_wait(barrier, bricks - 1)
    mine = ext.at[pl.ds(me * slots, slots)]
    for wave in range(len(WAVES)):
        for dx, dz in wave_offsets(wave):
            q = lax.rem(x + dx, NX) * NZ + lax.rem(z + dz, NZ)
            pltpu.make_async_remote_copy(
                src_ref=stage.at[pl.ds(q * slots, slots)], dst_ref=mine, send_sem=send_sem, recv_sem=recv_sems.at[wave],
                device_id={"brick": q}, device_id_type=MESH).start()
    lax.fori_loop(leaves // 8, leaves // 4, own, 0)
    def ghosts(q, source):
        for k in range(slots):
            prepare(source[q * slots + k], origin, feat, left, right, more, leaves + q * slots + k)
    ghosts(me, stage)
    for wave in range(len(WAVES)):
        count = len(wave_offsets(wave)) * slots
        pltpu.make_async_copy(stage.at[0:count], ext.at[0:count], recv_sems.at[wave]).wait()
        first, second = WAVES[wave]
        skip = 1 if first == 0 else 0
        def arrived(i, _):
            dz = first + (second - first) * (i // NX)
            q = lax.rem(x + NX - lax.rem(i, NX), NX) * NZ + lax.rem(z + NZ - dz, NZ)
            ghosts(q, ext)
            return 0
        lax.fori_loop(skip, count // slots + skip, arrived, 0)
    total = (bricks - 1) * slots
    pltpu.make_async_copy(stage.at[0:total], ext.at[0:total], send_sem).wait()

def back_kernel(bricks, slots, leaves, acc, back, send_sem, recv_sem):
    me, barrier = greet(bricks)
    rows = slice(0, 6)
    pl.semaphore_wait(barrier, bricks - 1)
    mine = back.at[pl.ds(me * slots, slots), rows]
    for wave in range(len(WAVES)):
        for dx, dz in wave_offsets(wave):
            q = lax.rem(me // NZ + dx, NX) * NZ + lax.rem(me + dz, NZ)
            pltpu.make_async_remote_copy(
                src_ref=acc.at[pl.ds(leaves + q * slots, slots), rows], dst_ref=mine, send_sem=send_sem, recv_sem=recv_sem,
                device_id={"brick": q}, device_id_type=MESH).start()
    back[pl.ds(me * slots, slots)] = acc[pl.ds(leaves + me * slots, slots)]
    total = (bricks - 1) * slots
    pltpu.make_async_copy(acc.at[0:total, rows], back.at[0:total, rows], recv_sem).wait()
    pltpu.make_async_copy(acc.at[0:total, rows], back.at[0:total, rows], send_sem).wait()

def tile_kernel(kept, kept_count, lent, plan, feat, left, right, more, acc, ids_a, ids_b,
                spread0, spread1, dots0, dots1, wide0, wide1, pend):
    region = lax.axis_index("region")
    spread0[...] = spread_matrix()
    spread1[...] = spread_matrix()
    acc[...] = jnp.zeros_like(acc)
    pend[...] = jnp.zeros_like(pend)
    n_kept = kept_count[0]
    def list_kept(i, _):
        ids_a[i] = kept[0, i]
        ids_b[i] = kept[1, i]
        return 0
    lax.fori_loop(0, n_kept, list_kept, 0)
    n = n_kept
    for j in range(plan.shape[1]):
        live = plan[region, j]
        def list_lent(i, first, j=j):
            ids_a[first + i] = lent[j, 0, i]
            ids_b[first + i] = lent[j, 1, i]
            return first
        lax.fori_loop(0, live, list_lent, n)
        n = n + live
    last = n - 1
    def at(t):
        t = jnp.minimum(t, last)
        return ids_a[t], ids_b[t]
    bufs = ((spread0, dots0, wide0), (spread1, dots1, wide1))
    products(*at(0), left, right, more, *bufs[0])
    lanes = lax.broadcasted_iota(jnp.int32, (8, 128), 1)
    diag = jnp.where(lanes % 8 == lax.broadcasted_iota(jnp.int32, (8, 128), 0), lanes // 8, -1)
    def tiles(first, count):
        for k in range(count):
            t = first + k
            a, b = at(t)
            products(*at(t + 1), left, right, more, *bufs[(k + 1) % 2])
            if k == 0:
                pending = [pend[q] for q in range(18)]
                before = at(jnp.maximum(t - 1, 0))
                live = True
            settle(pending, diag, acc, *before, live)
            pending = tile(b, feat, *bufs[k % 2][1:], diag)
            before = (a, b)
            live = t < n
        for q in range(18):
            pend[q] = jnp.where(live, pending[q], 0.0)
    def many(i, _):
        tiles(UNROLL * i, UNROLL)
        return 0
    def few(i, _):
        tiles(2 * i, 2)
        return 0
    whole = n // UNROLL
    lax.fori_loop(0, whole, many, 0)
    pairs = (n + 1) // 2
    lax.fori_loop(whole * (UNROLL // 2), pairs, few, 0)
    settle([pend[q] for q in range(18)], diag, acc, *at(2 * pairs - 1), True)

UNROLL = 4

def finish_kernel(slots, seg, ship, own, back, out, acc0, acc1, acc2, acc3):
    accs = (acc0, acc1, acc2, acc3)
    leaves = seg.shape[0]
    acc0[...] = own[0:leaves]
    for acc in accs[1:]:
        acc[...] = jnp.zeros_like(acc)
    bricks = back.shape[0] // slots
    for q in range(bricks):
        for k in range(slots):
            acc = accs[k % 4]
            leaf = ship[k, q]
            acc[leaf, 0:6] += back[q * slots + k, 0:6]
    for i in range(leaves):
        total = acc0[i] + acc1[i] + acc2[i] + acc3[i]
        d = [seg[i, 3 + q:4 + q] for q in range(3)]
        a = d[0] * d[0] + d[1] * d[1] + d[2] * d[2]
        inv = lax.rsqrt(a)
        half = 0.5 * (a * inv)
        u = [c * inv for c in d]
        force = [total[q:q + 1] for q in range(3)]
        lever = [total[3 + q:4 + q] - half * force[q] for q in range(3)]
        torque = [u[(q + 1) % 3] * lever[(q + 2) % 3] - u[(q + 2) % 3] * lever[(q + 1) % 3] for q in range(3)]
        for q in range(3):
            out[q, i:i + 1] = force[q]
            out[3 + q, i:i + 1] = torque[q]

VM = pl.BlockSpec(memory_space=pltpu.VMEM)
SM = pl.BlockSpec(memory_space=pltpu.SMEM)

def body(segments, ship_list, kept_tiles, kept_count, lent_tiles, lent_count):
    leaves, _, width = segments.shape
    bricks = lax.axis_size("brick")
    slots = ship_list.shape[2]
    ghosts = bricks * slots
    blocks = leaves + ghosts
    def shape(*s, dtype=F32):
        return jax.ShapeDtypeStruct(s, dtype)
    ship = jnp.transpose(ship_list[0], (1, 0))
    kept = jnp.transpose(kept_tiles[0], (1, 0))
    lent = jnp.transpose(lent_tiles[0], (0, 2, 1))
    prepared = pl.pallas_call(
        functools.partial(send_kernel, bricks, slots),
        out_shape=(shape(blocks, 8, width), shape(blocks, 128, 128, dtype=BF16), shape(blocks, 48, 384, dtype=BF16),
                   shape(blocks, 16, 768, dtype=BF16)),
        in_specs=[VM, SM], out_specs=(VM,) * 4,
        scratch_shapes=[pltpu.VMEM((ghosts, 8, width), F32), pltpu.VMEM((ghosts, 8, width), F32),
                        pltpu.SemaphoreType.DMA, pltpu.SemaphoreType.DMA((len(WAVES),))],
        compiler_params=pltpu.CompilerParams(collective_id=0, has_side_effects=True, vmem_limit_bytes=LIMIT),
    )(segments, ship)
    slots_total = kept_tiles.shape[1] + lent_tiles.shape[1] * lent_tiles.shape[2]
    acc = pl.pallas_call(
        tile_kernel,
        out_shape=shape(blocks, 8, width),
        in_specs=[SM] * 4 + [VM] * 4, out_specs=VM,
        scratch_shapes=[
            pltpu.SMEM((slots_total,), jnp.int32), pltpu.SMEM((slots_total,), jnp.int32),
            pltpu.VMEM((128, 1280), BF16), pltpu.VMEM((128, 1280), BF16),
            pltpu.VMEM((128, 384), F32), pltpu.VMEM((128, 384), F32),
            pltpu.VMEM((128, 1280), F32), pltpu.VMEM((128, 1280), F32),
            pltpu.VMEM((18, 8, 128), F32),
        ],
        compiler_params=pltpu.CompilerParams(vmem_limit_bytes=LIMIT),
    )(kept, kept_count, lent, lent_count[0], *prepared)
    back = pl.pallas_call(
        functools.partial(back_kernel, bricks, slots, leaves),
        out_shape=shape(ghosts, 8, width),
        in_specs=[VM], out_specs=VM,
        scratch_shapes=[pltpu.SemaphoreType.DMA, pltpu.SemaphoreType.DMA],
        compiler_params=pltpu.CompilerParams(collective_id=1, has_side_effects=True, vmem_limit_bytes=LIMIT),
    )(acc)
    loads = pl.pallas_call(
        functools.partial(finish_kernel, slots),
        out_shape=shape(6, leaves, width),
        in_specs=[VM, SM, VM, VM], out_specs=VM,
        scratch_shapes=[pltpu.VMEM((leaves, 8, width), F32)] * 4,
        compiler_params=pltpu.CompilerParams(vmem_limit_bytes=LIMIT),
    )(segments, ship, acc, back)
    return jnp.transpose(loads, (1, 0, 2))

LIMIT = 26 * 2**20

def solution(mesh):
    placed = (
        P(("brick", "region"), None, None),
        P(("brick", "region"), None, None),
        P(("brick", "region"), None, None),
        P(("brick", "region")),
        P(("brick", "region"), None, None, None),
        P("brick", None, None),
    )
    return jax.shard_map(body, mesh=mesh, in_specs=placed, out_specs=P(("brick", "region"), None, None), check_vma=False)
```

```python
import functools
import jax, jax.numpy as jnp
from jax import lax
from jax.experimental import pallas as pl
from jax.experimental.pallas import tpu as pltpu
from jax.sharding import PartitionSpec as P

MESH = pl.DeviceIdType.MESH
F32, BF16 = jnp.float32, jnp.bfloat16
DIST_FLOOR = 0.0025
PARALLEL_FLOOR = 0.05
TINY = 1e-20
LARGE = 1e30

def split3(x):
    hi = x.astype(BF16).astype(F32)
    rest = x - hi
    mid = rest.astype(BF16).astype(F32)
    return hi, mid, rest - mid

def prepare(seg, origin, feat, left, right, more, blk):
    p = seg[0:3] - origin
    d = seg[3:6]
    a = jnp.sum(d * d, axis=0, keepdims=True)
    inv = lax.rsqrt(a)
    u = d * inv
    length = a * inv
    along = jnp.sum(u * p, axis=0, keepdims=True)
    r = seg[6:7]
    ir = jnp.minimum(1.0 / r, LARGE)
    ie = jnp.minimum(0.75 / seg[7:8], LARGE)
    one = jnp.ones_like(r)
    x1 = jnp.concatenate([u, p, along, one], axis=0)
    x2 = jnp.concatenate([length, r, ir, ie, jnp.zeros((4, 128), F32)], axis=0)
    feat[blk] = jnp.concatenate([u, length, jnp.zeros((4, 128), F32)], axis=0)
    h1, m1, l1 = split3(x1)
    h2, m2, l2 = split3(x2)
    rows = jnp.concatenate([h1, h1, m1, m1, h1, l1, h2, m2, l2, jnp.ones((8, 128), F32), jnp.zeros((128 - 80, 128), F32)], axis=0)
    left[blk] = rows.T.astype(BF16)
    for q, x in enumerate(extra(p, r, ir, ie)):
        more[blk, :, 128 * q:128 * q + 128] = x
    z = jnp.zeros((3, 128), F32)
    z1 = jnp.zeros((1, 128), F32)
    for q, part in enumerate((
        jnp.concatenate([u, z, z1, z1], axis=0),
        jnp.concatenate([-p, z, one, z1], axis=0),
        jnp.concatenate([z, u, z1, -along], axis=0),
    )):
        h, m, l = split3(part)
        right[blk, :, 128 * q:128 * q + 128] = jnp.concatenate([h, m, h, m, l, h], axis=0).astype(BF16)
    return u, length

def extra(p, r, ir, ie):
    row = lax.broadcasted_iota(jnp.int32, (8, 128), 0)
    out = []
    for keep, x in ((-1, -p[0:1]), (-1, -p[1:2]), (-1, -p[2:3]), (1, r), (2, ir), (3, ie)):
        h, m, l = split3(x)
        out.append(jnp.concatenate([jnp.where(row == keep, 1.0, 0.0), h, m, l, jnp.zeros((5, 128), F32)], axis=0).astype(BF16))
    return out

def spread_matrix():
    row = lax.broadcasted_iota(jnp.int32, (128, 128), 0)
    cols = []
    for q in range(6):
        cols.append((row == q) | (row == 16 + q) | (row == 40 + q))
    for q in range(4):
        cols.append((row == 48 + q) | (row == 56 + q) | (row == 64 + q))
    return jnp.concatenate([jnp.where(c, 1.0, 0.0) for c in cols], axis=1).astype(BF16)

def products(a, b, left, right, more, spread, dots, wide):
    lhs = left[a]
    spread[64:80, 384:768] = more[b, :, 0:384]
    spread[64:80, 896:1280] = more[b, :, 384:768]
    dots[...] = jnp.dot(lhs[:, 0:48], right[b], preferred_element_type=F32)
    wide[...] = jnp.dot(lhs[:, 0:80], spread[0:80], preferred_element_type=F32)

def tile(b, feat, dots, wide, diag):
    def lane(q):
        return jnp.broadcast_to(feat[b, q:q + 1, :], (8, 128))
    u2 = [lane(q) for q in range(3)]
    len2 = lane(3)
    fsum = [None] * 6
    asum = [None] * 6
    for g in range(16):
        rs = slice(8 * g, 8 * g + 8)
        w, c, f = [dots[rs, 128 * q:128 * q + 128] for q in range(3)]
        wd = [wide[rs, 128 * q:128 * q + 128] for q in range(10)]
        u1, apart = wd[0:3], wd[3:6]
        len1, reach, ir, ie = wd[6:10]
        den = jnp.maximum(1.0 - w * w, PARALLEL_FLOOR)
        s = (w * f - c) * pltpu.reciprocal(den, approx=True)
        s = jnp.minimum(jnp.maximum(s, 0.0), len1)
        t = jnp.minimum(jnp.maximum(w * s + f, 0.0), len2)
        s = jnp.minimum(jnp.maximum(w * t - c, 0.0), len1)
        gap = [apart[q] + s * u1[q] - t * u2[q] for q in range(3)]
        m = jnp.maximum(gap[0] * gap[0] + gap[1] * gap[1] + gap[2] * gap[2], DIST_FLOOR)
        y = lax.rsqrt(m)
        h = jnp.maximum(reach - m * y, TINY)
        k = (h * h) * (lax.rsqrt(h * ir) * y) * pltpu.reciprocal(ie, approx=True)
        force = [k * x for x in gap]
        vals = force + [s * x for x in force]
        if g < 15:
            for q in range(6):
                red = jnp.sum(vals[q], axis=1, keepdims=True)
                asum[q] = jnp.where(diag == g, red, 0.0 if g == 0 else asum[q])
        back = force + [t * x for x in force]
        for q in range(6):
            fsum[q] = back[q] if g == 0 else fsum[q] + back[q]
    return vals + asum + fsum

def settle(pending, diag, acc, a, b, live):
    vals, asum, fsum = pending[0:6], pending[6:12], pending[12:18]
    for q in range(6):
        red = jnp.sum(vals[q], axis=1, keepdims=True)
        asum[q] = jnp.where(diag == 15, red, asum[q])
    for q in range(6):
        acc[q, pl.ds(a, 1), :] += jnp.where(live, jnp.sum(asum[q], axis=0, keepdims=True), 0.0)
    for q in range(6):
        acc[q, pl.ds(b, 1), :] -= jnp.where(live, jnp.sum(fsum[q], axis=0, keepdims=True), 0.0)


def greet(bricks):
    me = lax.axis_index("brick")
    barrier = pltpu.get_barrier_semaphore()
    for off in range(1, bricks):
        pl.semaphore_signal(barrier, inc=1, device_id={"brick": lax.rem(me + off, bricks)}, device_id_type=MESH)
    return me, barrier

WAVES = ((0, 0), (1, 7), (2, 6), (3, 5), (4, 4))
NX, NZ = 4, 8

def wave_offsets(wave):
    first, second = WAVES[wave]
    zs = (first,) if first == second else (first, second)
    return [(dx, dz) for dz in zs for dx in range(NX) if (dx, dz) != (0, 0)]

def over_lanes(x, y):
    return lax.dot_general(x.astype(BF16), y.astype(BF16), (((1,), (1,)), ((), ())), preferred_element_type=F32)

def make_lists(kept, kept_count, lent, plan, lists):
    region = lax.axis_index("region")
    slots, regions, lend = kept.shape[1], plan.shape[0], lent.shape[2]
    lane = lax.broadcasted_iota(jnp.int32, (1, slots), 1)
    live = [lane < kept_count[0]]
    ids = [[kept[0:1, :]], [kept[1:2, :]]]
    step = lax.broadcasted_iota(jnp.int32, (1, lend), 1)
    counts = plan[pl.ds(region, 1), :]
    for j in range(regions):
        live.append(step < jnp.broadcast_to(counts[:, j:j + 1], (1, lend)))
        for side in range(2):
            ids[side].append(lent[j, side:side + 1, :])
    def ones(x):
        return jnp.where(x, 1.0, 0.0)
    live = jnp.concatenate([ones(x) for x in live], axis=1)
    width = live.shape[1]
    first, second = [jnp.concatenate([x.astype(F32) for x in ids[side]], axis=1) for side in range(2)]
    row = lax.broadcasted_iota(jnp.int32, (width, width), 0)
    col = lax.broadcasted_iota(jnp.int32, (width, width), 1)
    wide = jnp.broadcast_to(live, (8, width))
    before = over_lanes(wide, ones(col < row))[0:1]
    total = over_lanes(wide, jnp.ones((width, width), F32))[0:1]
    place = jnp.where(live > 0.0, before, -1.0)
    pick = ones(jnp.broadcast_to(place, (width, width)).astype(jnp.int32) == row)
    rows = jnp.concatenate([first, second, jnp.zeros((6, width), F32)], axis=0)
    rows = over_lanes(rows, pick)
    out = jnp.concatenate([rows[0:2], total, jnp.zeros((5, width), F32)], axis=0)
    lists[...] = out.astype(jnp.int32)

def make_owner(ship, owner):
    leaves, ghosts = owner.shape
    slots, bricks = ship.shape
    leaf = lax.broadcasted_iota(jnp.int32, (leaves, bricks), 0)
    here = [jnp.where(jnp.broadcast_to(ship[k:k + 1, :], (leaves, bricks)) == leaf, 1.0, 0.0) for k in range(slots)]
    ghost = lax.broadcasted_iota(jnp.int32, (ghosts, bricks), 0)
    brick = lax.broadcasted_iota(jnp.int32, (ghosts, bricks), 1)
    total = 0.0
    for k in range(slots):
        total += over_lanes(here[k], jnp.where(ghost == brick * slots + k, 1.0, 0.0))
    owner[...] = total.astype(BF16)

def send_kernel(bricks, slots, seg_hbm, ship_hbm, kept_hbm, count, lent_hbm, plan_hbm,
                feat, left, right, more, lists, owner, axes,
                seg, ship, ship_rows, kept, lent, plan, ext, stage, in_sems, send_sem, recv_sems):
    pairs = ((seg_hbm, seg), (ship_hbm, ship), (ship_hbm, ship_rows), (kept_hbm, kept),
             (lent_hbm, lent), (plan_hbm, plan))
    copies = [pltpu.make_async_copy(src, dst, in_sems.at[i]) for i, (src, dst) in enumerate(pairs)]
    for copy in copies:
        copy.start()
    me, barrier = greet(bricks)
    x, z = me // NZ, lax.rem(me, NZ)
    leaves = seg.shape[0]
    for copy in copies[0:2]:
        copy.wait()
    for q in range(bricks):
        for k in range(slots):
            stage[q * slots + k] = seg[ship[k, q]]
    origin = jnp.broadcast_to(seg[0, 0:3, 0:1], (3, 128))
    def own(i, _):
        for k in range(4):
            j = 4 * i + k
            u, length = prepare(seg[j], origin, feat, left, right, more, j)
            for q in range(3):
                axes[q, pl.ds(j, 1), :] = u[q:q + 1]
            axes[3, pl.ds(j, 1), :] = length
        return 0
    lax.fori_loop(0, leaves // 8, own, 0)
    pl.semaphore_wait(barrier, bricks - 1)
    mine = ext.at[pl.ds(me * slots, slots)]
    for wave in range(len(WAVES)):
        for dx, dz in wave_offsets(wave):
            q = lax.rem(x + dx, NX) * NZ + lax.rem(z + dz, NZ)
            pltpu.make_async_remote_copy(
                src_ref=stage.at[pl.ds(q * slots, slots)], dst_ref=mine, send_sem=send_sem, recv_sem=recv_sems.at[wave],
                device_id={"brick": q}, device_id_type=MESH).start()
    lax.fori_loop(leaves // 8, leaves // 4, own, 0)
    def ghosts(q, source):
        for k in range(slots):
            prepare(source[q * slots + k], origin, feat, left, right, more, leaves + q * slots + k)
    ghosts(me, stage)
    for copy in copies[2:]:
        copy.wait()
    make_lists(kept, count, lent, plan, lists)
    make_owner(ship_rows, owner)
    for wave in range(len(WAVES)):
        count_in = len(wave_offsets(wave)) * slots
        pltpu.make_async_copy(stage.at[0:count_in], ext.at[0:count_in], recv_sems.at[wave]).wait()
        first, second = WAVES[wave]
        skip = 1 if first == 0 else 0
        def arrived(i, _):
            dz = first + (second - first) * (i // NX)
            q = lax.rem(x + NX - lax.rem(i, NX), NX) * NZ + lax.rem(z + NZ - dz, NZ)
            ghosts(q, ext)
            return 0
        lax.fori_loop(skip, count_in // slots + skip, arrived, 0)
    total = (bricks - 1) * slots
    pltpu.make_async_copy(stage.at[0:total], ext.at[0:total], send_sem).wait()

def back_kernel(bricks, slots, leaves, acc, back, send_sem, recv_sem):
    me, barrier = greet(bricks)
    pl.semaphore_wait(barrier, bricks - 1)
    mine = back.at[:, pl.ds(me * slots, slots)]
    for wave in range(len(WAVES)):
        for dx, dz in wave_offsets(wave):
            q = lax.rem(me // NZ + dx, NX) * NZ + lax.rem(me + dz, NZ)
            pltpu.make_async_remote_copy(
                src_ref=acc.at[:, pl.ds(leaves + q * slots, slots)], dst_ref=mine, send_sem=send_sem, recv_sem=recv_sem,
                device_id={"brick": q}, device_id_type=MESH).start()
    for q in range(6):
        back[q, pl.ds(me * slots, slots)] = acc[q, pl.ds(leaves + me * slots, slots)]
    total = (bricks - 1) * slots
    pltpu.make_async_copy(acc.at[:, 0:total], back.at[:, 0:total], recv_sem).wait()
    pltpu.make_async_copy(acc.at[:, 0:total], back.at[:, 0:total], send_sem).wait()

UNROLL = 4

def tile_kernel(lists, feat, left, right, more, acc, spread0, spread1, dots0, dots1, wide0, wide1, pend):
    n = lists[2, 0]
    last = n - 1
    def at(t):
        t = jnp.minimum(t, last)
        return lists[0, t], lists[1, t]
    spread0[...] = spread_matrix()
    spread1[...] = spread0[...]
    bufs = ((spread0, dots0, wide0), (spread1, dots1, wide1))
    products(*at(0), left, right, more, *bufs[0])
    acc[...] = jnp.zeros_like(acc)
    pend[...] = jnp.zeros_like(pend)
    lanes = lax.broadcasted_iota(jnp.int32, (8, 128), 1)
    diag = jnp.where(lanes % 8 == lax.broadcasted_iota(jnp.int32, (8, 128), 0), lanes // 8, -1)
    def tiles(first, count):
        for k in range(count):
            t = first + k
            a, b = at(t)
            products(*at(t + 1), left, right, more, *bufs[(k + 1) % 2])
            if k == 0:
                pending = [pend[q] for q in range(18)]
                before = at(jnp.maximum(t - 1, 0))
                live = True
            settle(pending, diag, acc, *before, live)
            pending = tile(b, feat, *bufs[k % 2][1:], diag)
            before = (a, b)
            live = t < n
        for q in range(18):
            pend[q] = jnp.where(live, pending[q], 0.0)
    def many(i, _):
        tiles(UNROLL * i, UNROLL)
        return 0
    def few(i, _):
        tiles(2 * i, 2)
        return 0
    whole = n // UNROLL
    lax.fori_loop(0, whole, many, 0)
    pairs = (n + 1) // 2
    lax.fori_loop(whole * (UNROLL // 2), pairs, few, 0)
    settle([pend[q] for q in range(18)], diag, acc, *at(2 * pairs - 1), True)

def finish_kernel(axes, owner, own, back, out):
    leaves = out.shape[1]
    pick = owner[...]
    pick = jnp.concatenate([pick, pick, pick], axis=1)
    total = []
    for q in range(6):
        parts = jnp.concatenate(split3(back[q]), axis=0).astype(BF16)
        total.append(own[q, 0:leaves] + jnp.dot(pick, parts, preferred_element_type=F32))
    u = [axes[q] for q in range(3)]
    half = 0.5 * axes[3]
    force = total[0:3]
    lever = [total[3 + q] - half * force[q] for q in range(3)]
    for q in range(3):
        out[q] = force[q]
        out[3 + q] = u[(q + 1) % 3] * lever[(q + 2) % 3] - u[(q + 2) % 3] * lever[(q + 1) % 3]

VM = pl.BlockSpec(memory_space=pltpu.VMEM)
SM = pl.BlockSpec(memory_space=pltpu.SMEM)
HB = pl.BlockSpec(memory_space=pltpu.HBM)
LIMIT = 26 * 2**20

def body(segments, ship_list, kept_tiles, kept_count, lent_tiles, lent_count):
    leaves, _, width = segments.shape
    bricks = lax.axis_size("brick")
    slots = ship_list.shape[2]
    ghosts = bricks * slots
    blocks = leaves + ghosts
    def shape(*s, dtype=F32):
        return jax.ShapeDtypeStruct(s, dtype)
    def far(x):
        return pltpu.with_memory_space_constraint(x, pltpu.HBM)
    def room(x):
        return pltpu.VMEM(x.shape, x.dtype)
    ship = jnp.transpose(ship_list[0], (1, 0))
    kept = jnp.transpose(kept_tiles[0], (1, 0))
    lent = jnp.transpose(lent_tiles[0], (0, 2, 1))
    tile_slots = kept_tiles.shape[1] + lent_tiles.shape[1] * lent_tiles.shape[2]
    feat, left, right, more, lists, owner, axes = pl.pallas_call(
        functools.partial(send_kernel, bricks, slots),
        out_shape=(shape(blocks, 8, width), shape(blocks, 128, 128, dtype=BF16), shape(blocks, 48, 384, dtype=BF16),
                   shape(blocks, 16, 768, dtype=BF16), shape(8, tile_slots, dtype=jnp.int32),
                   shape(leaves, ghosts, dtype=BF16), shape(4, leaves, width)),
        in_specs=[HB] * 3 + [SM] + [HB] * 2, out_specs=(VM,) * 7,
        scratch_shapes=[room(segments), pltpu.SMEM(ship.shape, jnp.int32), room(ship), room(kept), room(lent),
                        pltpu.VMEM(lent_count.shape[1:], jnp.int32),
                        pltpu.VMEM((ghosts, 8, width), F32), pltpu.VMEM((ghosts, 8, width), F32),
                        pltpu.SemaphoreType.DMA((6,)), pltpu.SemaphoreType.DMA, pltpu.SemaphoreType.DMA((len(WAVES),))],
        compiler_params=pltpu.CompilerParams(collective_id=0, has_side_effects=True, vmem_limit_bytes=LIMIT),
    )(far(segments), far(ship), far(kept), kept_count, far(lent), far(lent_count[0]))
    acc = pl.pallas_call(
        tile_kernel,
        out_shape=shape(6, blocks, width),
        in_specs=[SM] + [VM] * 4, out_specs=VM,
        scratch_shapes=[
            pltpu.VMEM((128, 1280), BF16), pltpu.VMEM((128, 1280), BF16),
            pltpu.VMEM((128, 384), F32), pltpu.VMEM((128, 384), F32),
            pltpu.VMEM((128, 1280), F32), pltpu.VMEM((128, 1280), F32),
            pltpu.VMEM((18, 8, 128), F32),
        ],
        compiler_params=pltpu.CompilerParams(vmem_limit_bytes=LIMIT),
    )(lists, feat, left, right, more)
    back = pl.pallas_call(
        functools.partial(back_kernel, bricks, slots, leaves),
        out_shape=shape(6, ghosts, width),
        in_specs=[VM], out_specs=VM,
        scratch_shapes=[pltpu.SemaphoreType.DMA, pltpu.SemaphoreType.DMA],
        compiler_params=pltpu.CompilerParams(collective_id=1, has_side_effects=True, vmem_limit_bytes=LIMIT),
    )(acc)
    loads = pl.pallas_call(
        finish_kernel,
        out_shape=shape(6, leaves, width),
        in_specs=[VM] * 4, out_specs=VM,
        compiler_params=pltpu.CompilerParams(vmem_limit_bytes=LIMIT),
    )(axes, owner, acc, back)
    return jnp.transpose(loads, (1, 0, 2))

def solution(mesh):
    placed = (
        P(("brick", "region"), None, None),
        P(("brick", "region"), None, None),
        P(("brick", "region"), None, None),
        P(("brick", "region")),
        P(("brick", "region"), None, None, None),
        P("brick", None, None),
    )
    return jax.shard_map(body, mesh=mesh, in_specs=placed, out_specs=P(("brick", "region"), None, None), check_vma=False)
```

```python
import functools
import jax, jax.numpy as jnp
from jax import lax
from jax.experimental import pallas as pl
from jax.experimental.pallas import tpu as pltpu
from jax.sharding import PartitionSpec as P

MESH = pl.DeviceIdType.MESH
F32, BF16 = jnp.float32, jnp.bfloat16
DIST_FLOOR = 0.0025
PARALLEL_FLOOR = 0.05
TINY = 1e-20
LARGE = 1e30

def split3(x):
    hi = x.astype(BF16).astype(F32)
    rest = x - hi
    mid = rest.astype(BF16).astype(F32)
    return hi, mid, rest - mid

def prepare(seg, origin, feat, left, right, more, blk):
    p = seg[0:3] - origin
    d = seg[3:6]
    a = jnp.sum(d * d, axis=0, keepdims=True)
    inv = lax.rsqrt(a)
    u = d * inv
    length = a * inv
    along = jnp.sum(u * p, axis=0, keepdims=True)
    r = seg[6:7]
    ir = jnp.minimum(1.0 / r, LARGE)
    ie = jnp.minimum(0.75 / seg[7:8], LARGE)
    one = jnp.ones_like(r)
    x1 = jnp.concatenate([u, p, along, one], axis=0)
    x2 = jnp.concatenate([length, r, ir, ie, jnp.zeros((4, 128), F32)], axis=0)
    feat[blk] = jnp.concatenate([u, length, jnp.zeros((4, 128), F32)], axis=0)
    h1, m1, l1 = split3(x1)
    h2, m2, l2 = split3(x2)
    rows = jnp.concatenate([h1, h1, m1, m1, h1, l1, h2, m2, l2, jnp.ones((8, 128), F32), jnp.zeros((128 - 80, 128), F32)], axis=0)
    left[blk] = rows.T.astype(BF16)
    for q, x in enumerate(extra(p, r, ir, ie)):
        more[blk, :, 128 * q:128 * q + 128] = x
    z = jnp.zeros((3, 128), F32)
    z1 = jnp.zeros((1, 128), F32)
    for q, part in enumerate((
        jnp.concatenate([u, z, z1, z1], axis=0),
        jnp.concatenate([-p, z, one, z1], axis=0),
        jnp.concatenate([z, u, z1, -along], axis=0),
    )):
        h, m, l = split3(part)
        right[blk, :, 128 * q:128 * q + 128] = jnp.concatenate([h, m, h, m, l, h], axis=0).astype(BF16)
    return u, length

def extra(p, r, ir, ie):
    row = lax.broadcasted_iota(jnp.int32, (8, 128), 0)
    out = []
    for keep, x in ((-1, -p[0:1]), (-1, -p[1:2]), (-1, -p[2:3]), (1, r), (2, ir), (3, ie)):
        h, m, l = split3(x)
        out.append(jnp.concatenate([jnp.where(row == keep, 1.0, 0.0), h, m, l, jnp.zeros((5, 128), F32)], axis=0).astype(BF16))
    return out

def spread_matrix():
    row = lax.broadcasted_iota(jnp.int32, (128, 128), 0)
    cols = []
    for q in range(6):
        cols.append((row == q) | (row == 16 + q) | (row == 40 + q))
    for q in range(4):
        cols.append((row == 48 + q) | (row == 56 + q) | (row == 64 + q))
    return jnp.concatenate([jnp.where(c, 1.0, 0.0) for c in cols], axis=1).astype(BF16)

def products(a, b, left, right, more, spread, dots, wide):
    lhs = left[a]
    spread[64:80, 384:768] = more[b, :, 0:384]
    spread[64:80, 896:1280] = more[b, :, 384:768]
    dots[...] = jnp.dot(lhs[:, 0:48], right[b], preferred_element_type=F32)
    wide[...] = jnp.dot(lhs[:, 0:80], spread[0:80], preferred_element_type=F32)

def tile(b, feat, dots, wide, diag):
    def lane(q):
        return jnp.broadcast_to(feat[b, q:q + 1, :], (8, 128))
    u2 = [lane(q) for q in range(3)]
    len2 = lane(3)
    fsum = [None] * 6
    asum = [None] * 6
    for g in range(16):
        rs = slice(8 * g, 8 * g + 8)
        w, c, f = [dots[rs, 128 * q:128 * q + 128] for q in range(3)]
        wd = [wide[rs, 128 * q:128 * q + 128] for q in range(10)]
        u1, apart = wd[0:3], wd[3:6]
        len1, reach, ir, ie = wd[6:10]
        den = jnp.maximum(1.0 - w * w, PARALLEL_FLOOR)
        s = (w * f - c) * pltpu.reciprocal(den, approx=True)
        s = jnp.minimum(jnp.maximum(s, 0.0), len1)
        t = jnp.minimum(jnp.maximum(w * s + f, 0.0), len2)
        s = jnp.minimum(jnp.maximum(w * t - c, 0.0), len1)
        gap = [apart[q] + s * u1[q] - t * u2[q] for q in range(3)]
        m = jnp.maximum(gap[0] * gap[0] + gap[1] * gap[1] + gap[2] * gap[2], DIST_FLOOR)
        y = lax.rsqrt(m)
        h = jnp.maximum(reach - m * y, TINY)
        k = (h * h) * (lax.rsqrt(h * ir) * y) * pltpu.reciprocal(ie, approx=True)
        force = [k * x for x in gap]
        vals = force + [s * x for x in force]
        if g < 15:
            for q in range(6):
                red = jnp.sum(vals[q], axis=1, keepdims=True)
                asum[q] = jnp.where(diag == g, red, 0.0 if g == 0 else asum[q])
        back = force + [t * x for x in force]
        for q in range(6):
            fsum[q] = back[q] if g == 0 else fsum[q] + back[q]
    return vals + asum + fsum

def diagonal():
    lanes = lax.broadcasted_iota(jnp.int32, (8, 128), 1)
    return jnp.where(lanes % 8 == lax.broadcasted_iota(jnp.int32, (8, 128), 0), lanes // 8, -1)

def reduced(pending, diag):
    vals, asum, fsum = pending[0:6], pending[6:12], pending[12:18]
    last = [jnp.where(diag == 15, jnp.sum(vals[q], axis=1, keepdims=True), asum[q]) for q in range(6)]
    return [jnp.sum(x, axis=0, keepdims=True) for x in last], [jnp.sum(x, axis=0, keepdims=True) for x in fsum]

def settle(pending, diag, acc, a, b, live):
    asum, fsum = reduced(pending, diag)
    for q in range(6):
        acc[q, pl.ds(a, 1), :] += jnp.where(live, asum[q], 0.0)
    for q in range(6):
        acc[q, pl.ds(b, 1), :] -= jnp.where(live, fsum[q], 0.0)

def greet(bricks):
    me = lax.axis_index("brick")
    barrier = pltpu.get_barrier_semaphore()
    for off in range(1, bricks):
        pl.semaphore_signal(barrier, inc=1, device_id={"brick": lax.rem(me + off, bricks)}, device_id_type=MESH)
    return me, barrier

WAVES = ((0, 0), (1, 7), (2, 6), (3, 5), (4, 4))
NX, NZ = 4, 8

def wave_offsets(wave):
    first, second = WAVES[wave]
    zs = (first,) if first == second else (first, second)
    return [(dx, dz) for dz in zs for dx in range(NX) if (dx, dz) != (0, 0)]

def over_lanes(x, y):
    return lax.dot_general(x.astype(BF16), y.astype(BF16), (((1,), (1,)), ((), ())), preferred_element_type=F32)

LATE = 24

def make_lists(leaves, slots_out, kept, kept_count, lent, plan, lists):
    region = lax.axis_index("region")
    slots, regions, lend = kept.shape[1], plan.shape[0], lent.shape[2]
    lane = lax.broadcasted_iota(jnp.int32, (1, slots), 1)
    live = [lane < kept_count[0]]
    ids = [[kept[0:1, :]], [kept[1:2, :]]]
    step = lax.broadcasted_iota(jnp.int32, (1, lend), 1)
    counts = plan[pl.ds(region, 1), :]
    for j in range(regions):
        live.append(step < jnp.broadcast_to(counts[:, j:j + 1], (1, lend)))
        for side in range(2):
            ids[side].append(lent[j, side:side + 1, :])
    def ones(x):
        return jnp.where(x, 1.0, 0.0)
    live = jnp.concatenate([ones(x) for x in live], axis=1)
    width = live.shape[1]
    first, second = [jnp.concatenate([x.astype(F32) for x in ids[side]], axis=1) for side in range(2)]
    row = lax.broadcasted_iota(jnp.int32, (width, width), 0)
    col = lax.broadcasted_iota(jnp.int32, (width, width), 1)
    def inner(v):
        return jnp.where((v >= leaves) & (lax.rem(v, slots_out) >= slots_out // 2), 0.0, 1.0)
    inside = live * inner(first.astype(jnp.int32)) * inner(second.astype(jnp.int32))
    def before(flags):
        return over_lanes(jnp.broadcast_to(flags, (8, width)), ones(col < row))[0:1]
    late = jnp.where(before(inside) < LATE, inside, 0.0)
    now = live - late
    total = over_lanes(jnp.broadcast_to(now, (8, width)), jnp.ones((width, width), F32))[0:1]
    def moved(values, flags, shift):
        place = jnp.where(flags > 0.0, before(flags) + shift, -1.0).astype(jnp.int32)
        pick = ones(jnp.broadcast_to(place, (width, width)) == row)
        return over_lanes(jnp.broadcast_to(values, (8, width)), pick)[0:1]
    late_a, late_b = moved(first + 1.0, late, 1), moved(second + 1.0, late, 1)
    places = late_a + moved(second + 1.0, late, 1 + width // 2) - 1.0
    out = jnp.concatenate([moved(first, now, 0), moved(second, now, 0), total, jnp.maximum(late_a - 1.0, 0.0),
                           jnp.maximum(late_b - 1.0, 0.0), places, jnp.zeros((2, width), F32)], axis=0)
    lists[...] = out.astype(jnp.int32)

def make_owner(ship, owner):
    leaves, ghosts = owner.shape
    slots, bricks = ship.shape
    leaf = lax.broadcasted_iota(jnp.int32, (leaves, bricks), 0)
    here = [jnp.where(jnp.broadcast_to(ship[k:k + 1, :], (leaves, bricks)) == leaf, 1.0, 0.0) for k in range(slots)]
    ghost = lax.broadcasted_iota(jnp.int32, (ghosts, bricks), 0)
    brick = lax.broadcasted_iota(jnp.int32, (ghosts, bricks), 1)
    total = 0.0
    for k in range(slots):
        total += over_lanes(here[k], jnp.where(ghost == brick * slots + k, 1.0, 0.0))
    owner[...] = total.astype(BF16)

def send_kernel(bricks, slots, seg_hbm, ship_hbm, kept_hbm, count, lent_hbm, plan_hbm,
                feat, left, right, more, lists, owner, axes,
                seg, ship, ship_rows, kept, lent, plan, ext, stage, in_sems, send_sem, recv_sems):
    pairs = ((seg_hbm, seg), (ship_hbm, ship), (ship_hbm, ship_rows), (kept_hbm, kept),
             (lent_hbm, lent), (plan_hbm, plan))
    copies = [pltpu.make_async_copy(src, dst, in_sems.at[i]) for i, (src, dst) in enumerate(pairs)]
    for copy in copies:
        copy.start()
    me, barrier = greet(bricks)
    x, z = me // NZ, lax.rem(me, NZ)
    leaves = seg.shape[0]
    for copy in copies[0:2]:
        copy.wait()
    for q in range(bricks):
        for k in range(slots):
            stage[q * slots + k] = seg[ship[k, q]]
    origin = jnp.broadcast_to(seg[0, 0:3, 0:1], (3, 128))
    def own(i, _):
        for k in range(4):
            j = 4 * i + k
            u, length = prepare(seg[j], origin, feat, left, right, more, j)
            for q in range(3):
                axes[q, pl.ds(j, 1), :] = u[q:q + 1]
            axes[3, pl.ds(j, 1), :] = length
        return 0
    lax.fori_loop(0, leaves // 8, own, 0)
    pl.semaphore_wait(barrier, bricks - 1)
    mine = ext.at[pl.ds(me * slots, slots)]
    for wave in range(len(WAVES)):
        for dx, dz in wave_offsets(wave):
            q = lax.rem(x + dx, NX) * NZ + lax.rem(z + dz, NZ)
            pltpu.make_async_remote_copy(
                src_ref=stage.at[pl.ds(q * slots, slots)], dst_ref=mine, send_sem=send_sem, recv_sem=recv_sems.at[wave],
                device_id={"brick": q}, device_id_type=MESH).start()
    lax.fori_loop(leaves // 8, leaves // 4, own, 0)
    def ghosts(q, source):
        for k in range(slots):
            prepare(source[q * slots + k], origin, feat, left, right, more, leaves + q * slots + k)
    ghosts(me, stage)
    for copy in copies[2:]:
        copy.wait()
    make_lists(leaves, slots, kept, count, lent, plan, lists)
    make_owner(ship_rows, owner)
    for wave in range(len(WAVES)):
        count_in = len(wave_offsets(wave)) * slots
        pltpu.make_async_copy(stage.at[0:count_in], ext.at[0:count_in], recv_sems.at[wave]).wait()
        first, second = WAVES[wave]
        skip = 1 if first == 0 else 0
        def arrived(i, _):
            dz = first + (second - first) * (i // NX)
            q = lax.rem(x + NX - lax.rem(i, NX), NX) * NZ + lax.rem(z + NZ - dz, NZ)
            ghosts(q, ext)
            return 0
        lax.fori_loop(skip, count_in // slots + skip, arrived, 0)
    total = (bricks - 1) * slots
    pltpu.make_async_copy(stage.at[0:total], ext.at[0:total], send_sem).wait()

def back_kernel(bricks, slots, leaves, lists, places, feat, left, right, more, acc, own, back, total, sums,
                spread0, spread1, dots0, dots1, wide0, wide1, pend, send_sem, recv_sems):
    me, barrier = greet(bricks)
    def at(t):
        t = jnp.minimum(t + 1, LATE)
        return lists[3, t], lists[4, t]
    spread0[...] = spread_matrix()
    spread1[...] = spread0[...]
    bufs = ((spread0, dots0, wide0), (spread1, dots1, wide1))
    products(*at(0), left, right, more, *bufs[0])
    pend[...] = jnp.zeros_like(pend)
    sums[...] = jnp.zeros_like(sums)
    diag = diagonal()
    def keep(pending, row):
        asum, fsum = reduced(pending, diag)
        for q in range(6):
            sums[q, pl.ds(row, 1), :] = asum[q]
            sums[q, pl.ds(row + 64, 1), :] = -fsum[q]
    def some(i, _):
        for k in range(LATE_UNROLL):
            t = LATE_UNROLL * i + k
            _, b = at(t)
            products(*at(t + 1), left, right, more, *bufs[(k + 1) % 2])
            if k == 0:
                pending = [pend[q] for q in range(18)]
            keep(pending, t)
            pending = tile(b, feat, *bufs[k % 2][1:], diag)
        for q in range(18):
            pend[q] = pending[q]
        return 0
    half = slots // 2
    def send(half_number, source):
        mine = back.at[:, pl.ds(me * slots + half_number * half, half)]
        for wave in range(len(WAVES)):
            for dx, dz in wave_offsets(wave):
                q = lax.rem(me // NZ + dx, NX) * NZ + lax.rem(me + dz, NZ)
                pltpu.make_async_remote_copy(
                    src_ref=source.at[:, pl.ds(leaves + q * slots + half_number * half, half)], dst_ref=mine,
                    send_sem=send_sem, recv_sem=recv_sems.at[half_number], device_id={"brick": q}, device_id_type=MESH).start()
    lax.fori_loop(0, EARLY // LATE_UNROLL, some, 0)
    pl.semaphore_wait(barrier, bricks - 1)
    send(1, acc)
    lax.fori_loop(EARLY // LATE_UNROLL, LATE // LATE_UNROLL, some, 0)
    keep([pend[q] for q in range(18)], LATE)
    blocks = total.shape[1]
    pick = jnp.where(lax.broadcasted_iota(jnp.int32, (blocks, 128), 0) == jnp.broadcast_to(places[5:6, :], (blocks, 128)), 1.0, 0.0)
    pick = pick.astype(BF16)
    pick = jnp.concatenate([pick, pick, pick], axis=1)
    for q in range(6):
        parts = jnp.concatenate(split3(sums[q]), axis=0).astype(BF16)
        total[q] = acc[q] + jnp.dot(pick, parts, preferred_element_type=F32)
    send(0, total)
    own[...] = total[:, 0:leaves]
    for q in range(6):
        back[q, pl.ds(me * slots, half)] = total[q, pl.ds(leaves + me * slots, half)]
        back[q, pl.ds(me * slots + half, half)] = acc[q, pl.ds(leaves + me * slots + half, half)]
    sent = (bricks - 1) * half
    for half_number in range(2):
        pltpu.make_async_copy(acc.at[:, 0:sent], back.at[:, 0:sent], recv_sems.at[half_number]).wait()
    pltpu.make_async_copy(acc.at[:, 0:2 * sent], back.at[:, 0:2 * sent], send_sem).wait()

LATE_UNROLL = 4
EARLY = 8
UNROLL = 4

def tile_kernel(lists, feat, left, right, more, acc, spread0, spread1, dots0, dots1, wide0, wide1, pend):
    n = lists[2, 0]
    last = jnp.maximum(n - 1, 0)
    def at(t):
        t = jnp.minimum(jnp.maximum(t, 0), last)
        return lists[0, t], lists[1, t]
    spread0[...] = spread_matrix()
    spread1[...] = spread0[...]
    bufs = ((spread0, dots0, wide0), (spread1, dots1, wide1))
    products(*at(0), left, right, more, *bufs[0])
    acc[...] = jnp.zeros_like(acc)
    pend[...] = jnp.zeros_like(pend)
    diag = diagonal()
    def tiles(first, count):
        for k in range(count):
            t = first + k
            a, b = at(t)
            products(*at(t + 1), left, right, more, *bufs[(k + 1) % 2])
            if k == 0:
                pending = [pend[q] for q in range(18)]
                before = at(t - 1)
                live = True
            settle(pending, diag, acc, *before, live)
            pending = tile(b, feat, *bufs[k % 2][1:], diag)
            before = (a, b)
            live = t < n
        for q in range(18):
            pend[q] = jnp.where(live, pending[q], 0.0)
    def many(i, _):
        tiles(UNROLL * i, UNROLL)
        return 0
    def few(i, _):
        tiles(2 * i, 2)
        return 0
    whole = n // UNROLL
    lax.fori_loop(0, whole, many, 0)
    pairs = (n + 1) // 2
    lax.fori_loop(whole * (UNROLL // 2), pairs, few, 0)
    settle([pend[q] for q in range(18)], diag, acc, *at(2 * pairs - 1), True)

def finish_kernel(axes, owner, own, back, out):
    leaves = out.shape[1]
    pick = owner[...]
    pick = jnp.concatenate([pick, pick, pick], axis=1)
    total = []
    for q in range(6):
        parts = jnp.concatenate(split3(back[q]), axis=0).astype(BF16)
        total.append(own[q] + jnp.dot(pick, parts, preferred_element_type=F32))
    u = [axes[q] for q in range(3)]
    half = 0.5 * axes[3]
    force = total[0:3]
    lever = [total[3 + q] - half * force[q] for q in range(3)]
    for q in range(3):
        out[q] = force[q]
        out[3 + q] = u[(q + 1) % 3] * lever[(q + 2) % 3] - u[(q + 2) % 3] * lever[(q + 1) % 3]

VM = pl.BlockSpec(memory_space=pltpu.VMEM)
SM = pl.BlockSpec(memory_space=pltpu.SMEM)
HB = pl.BlockSpec(memory_space=pltpu.HBM)
LIMIT = 26 * 2**20

def body(segments, ship_list, kept_tiles, kept_count, lent_tiles, lent_count):
    leaves, _, width = segments.shape
    bricks = lax.axis_size("brick")
    slots = ship_list.shape[2]
    ghosts = bricks * slots
    blocks = leaves + ghosts
    def shape(*s, dtype=F32):
        return jax.ShapeDtypeStruct(s, dtype)
    def far(x):
        return pltpu.with_memory_space_constraint(x, pltpu.HBM)
    def room(x):
        return pltpu.VMEM(x.shape, x.dtype)
    ship = jnp.transpose(ship_list[0], (1, 0))
    kept = jnp.transpose(kept_tiles[0], (1, 0))
    lent = jnp.transpose(lent_tiles[0], (0, 2, 1))
    tile_slots = kept_tiles.shape[1] + lent_tiles.shape[1] * lent_tiles.shape[2]
    feat, left, right, more, lists, owner, axes = pl.pallas_call(
        functools.partial(send_kernel, bricks, slots),
        out_shape=(shape(blocks, 8, width), shape(blocks, 128, 128, dtype=BF16), shape(blocks, 48, 384, dtype=BF16),
                   shape(blocks, 16, 768, dtype=BF16), shape(8, tile_slots, dtype=jnp.int32),
                   shape(leaves, ghosts, dtype=BF16), shape(4, leaves, width)),
        in_specs=[HB] * 3 + [SM] + [HB] * 2, out_specs=(VM,) * 7,
        scratch_shapes=[room(segments), pltpu.SMEM(ship.shape, jnp.int32), room(ship), room(kept), room(lent),
                        pltpu.VMEM(lent_count.shape[1:], jnp.int32),
                        pltpu.VMEM((ghosts, 8, width), F32), pltpu.VMEM((ghosts, 8, width), F32),
                        pltpu.SemaphoreType.DMA((6,)), pltpu.SemaphoreType.DMA, pltpu.SemaphoreType.DMA((len(WAVES),))],
        compiler_params=pltpu.CompilerParams(collective_id=0, has_side_effects=True, vmem_limit_bytes=LIMIT),
    )(far(segments), far(ship), far(kept), kept_count, far(lent), far(lent_count[0]))
    buffers = [
        pltpu.VMEM((128, 1280), BF16), pltpu.VMEM((128, 1280), BF16),
        pltpu.VMEM((128, 384), F32), pltpu.VMEM((128, 384), F32),
        pltpu.VMEM((128, 1280), F32), pltpu.VMEM((128, 1280), F32),
        pltpu.VMEM((18, 8, 128), F32),
    ]
    acc = pl.pallas_call(
        tile_kernel,
        out_shape=shape(6, blocks, width),
        in_specs=[SM] + [VM] * 4, out_specs=VM,
        scratch_shapes=buffers,
        compiler_params=pltpu.CompilerParams(vmem_limit_bytes=LIMIT),
    )(lists, feat, left, right, more)
    own, back = pl.pallas_call(
        functools.partial(back_kernel, bricks, slots, leaves),
        out_shape=(shape(6, leaves, width), shape(6, ghosts, width)),
        in_specs=[SM] + [VM] * 6, out_specs=(VM, VM),
        scratch_shapes=[pltpu.VMEM((6, blocks, width), F32), pltpu.VMEM((6, 128, width), F32)] + buffers
        + [pltpu.SemaphoreType.DMA, pltpu.SemaphoreType.DMA((2,))],
        compiler_params=pltpu.CompilerParams(collective_id=1, has_side_effects=True, vmem_limit_bytes=LIMIT),
    )(lists, lists, feat, left, right, more, acc)
    loads = pl.pallas_call(
        finish_kernel,
        out_shape=shape(6, leaves, width),
        in_specs=[VM] * 4, out_specs=VM,
        compiler_params=pltpu.CompilerParams(vmem_limit_bytes=LIMIT),
    )(axes, owner, own, back)
    return jnp.transpose(loads, (1, 0, 2))

def solution(mesh):
    placed = (
        P(("brick", "region"), None, None),
        P(("brick", "region"), None, None),
        P(("brick", "region"), None, None),
        P(("brick", "region")),
        P(("brick", "region"), None, None, None),
        P("brick", None, None),
    )
    return jax.shard_map(body, mesh=mesh, in_specs=placed, out_specs=P(("brick", "region"), None, None), check_vma=False)
```

```python
import functools
import jax, jax.numpy as jnp
from jax import lax
from jax.experimental import pallas as pl
from jax.experimental.pallas import tpu as pltpu
from jax.sharding import PartitionSpec as P

MESH = pl.DeviceIdType.MESH
F32, BF16 = jnp.float32, jnp.bfloat16
DIST_FLOOR = 0.0025
PARALLEL_FLOOR = 0.05
TINY = 1e-20
LARGE = 1e30

def split3(x):
    hi = x.astype(BF16).astype(F32)
    rest = x - hi
    mid = rest.astype(BF16).astype(F32)
    return hi, mid, rest - mid

def prepare(seg, origin, feat, left, right, more, blk):
    p = seg[0:3] - origin
    d = seg[3:6]
    a = jnp.sum(d * d, axis=0, keepdims=True)
    inv = lax.rsqrt(a)
    u = d * inv
    length = a * inv
    along = jnp.sum(u * p, axis=0, keepdims=True)
    r = seg[6:7]
    ir = jnp.minimum(1.0 / r, LARGE)
    ie = jnp.minimum(0.75 / seg[7:8], LARGE)
    one = jnp.ones_like(r)
    x1 = jnp.concatenate([u, p, along, one], axis=0)
    x2 = jnp.concatenate([length, r, ir, ie, jnp.zeros((4, 128), F32)], axis=0)
    feat[blk] = jnp.concatenate([u, length, jnp.zeros((4, 128), F32)], axis=0)
    h1, m1, l1 = split3(x1)
    h2, m2, l2 = split3(x2)
    rows = jnp.concatenate([h1, h1, m1, m1, h1, l1, h2, m2, l2, jnp.ones((8, 128), F32), jnp.zeros((128 - 80, 128), F32)], axis=0)
    left[blk] = rows.T.astype(BF16)
    for q, x in enumerate(extra(p, r, ir, ie)):
        more[blk, :, 128 * q:128 * q + 128] = x
    z = jnp.zeros((3, 128), F32)
    z1 = jnp.zeros((1, 128), F32)
    for q, part in enumerate((
        jnp.concatenate([u, z, z1, z1], axis=0),
        jnp.concatenate([-p, z, one, z1], axis=0),
        jnp.concatenate([z, u, z1, -along], axis=0),
    )):
        h, m, l = split3(part)
        right[blk, :, 128 * q:128 * q + 128] = jnp.concatenate([h, m, h, m, l, h], axis=0).astype(BF16)
    return u, length

def extra(p, r, ir, ie):
    row = lax.broadcasted_iota(jnp.int32, (8, 128), 0)
    out = []
    for keep, x in ((-1, -p[0:1]), (-1, -p[1:2]), (-1, -p[2:3]), (1, r), (2, ir), (3, ie)):
        h, m, l = split3(x)
        out.append(jnp.concatenate([jnp.where(row == keep, 1.0, 0.0), h, m, l, jnp.zeros((5, 128), F32)], axis=0).astype(BF16))
    return out

def spread_matrix():
    row = lax.broadcasted_iota(jnp.int32, (128, 128), 0)
    cols = []
    for q in range(6):
        cols.append((row == q) | (row == 16 + q) | (row == 40 + q))
    for q in range(4):
        cols.append((row == 48 + q) | (row == 56 + q) | (row == 64 + q))
    return jnp.concatenate([jnp.where(c, 1.0, 0.0) for c in cols], axis=1).astype(BF16)

def products(a, b, left, right, more, spread, dots, wide):
    lhs = left[a]
    spread[64:80, 384:768] = more[b, :, 0:384]
    spread[64:80, 896:1280] = more[b, :, 384:768]
    dots[...] = jnp.dot(lhs[:, 0:48], right[b], preferred_element_type=F32)
    wide[...] = jnp.dot(lhs[:, 0:80], spread[0:80], preferred_element_type=F32)

def tile(b, feat, dots, wide, diag):
    def lane(q):
        return jnp.broadcast_to(feat[b, q:q + 1, :], (8, 128))
    u2 = [lane(q) for q in range(3)]
    len2 = lane(3)
    fsum = [None] * 6
    asum = [None] * 6
    for g in range(16):
        rs = slice(8 * g, 8 * g + 8)
        w, c, f = [dots[rs, 128 * q:128 * q + 128] for q in range(3)]
        wd = [wide[rs, 128 * q:128 * q + 128] for q in range(10)]
        u1, apart = wd[0:3], wd[3:6]
        len1, reach, ir, ie = wd[6:10]
        den = jnp.maximum(1.0 - w * w, PARALLEL_FLOOR)
        s = (w * f - c) * pltpu.reciprocal(den, approx=True)
        s = jnp.minimum(jnp.maximum(s, 0.0), len1)
        t = jnp.minimum(jnp.maximum(w * s + f, 0.0), len2)
        s = jnp.minimum(jnp.maximum(w * t - c, 0.0), len1)
        gap = [apart[q] + s * u1[q] - t * u2[q] for q in range(3)]
        m = jnp.maximum(gap[0] * gap[0] + gap[1] * gap[1] + gap[2] * gap[2], DIST_FLOOR)
        y = lax.rsqrt(m)
        h = jnp.maximum(reach - m * y, TINY)
        k = (h * h) * (lax.rsqrt(h * ir) * y) * pltpu.reciprocal(ie, approx=True)
        force = [k * x for x in gap]
        vals = force + [s * x for x in force]
        if g < 15:
            for q in range(6):
                red = jnp.sum(vals[q], axis=1, keepdims=True)
                asum[q] = jnp.where(diag == g, red, 0.0 if g == 0 else asum[q])
        back = force + [t * x for x in force]
        for q in range(6):
            fsum[q] = back[q] if g == 0 else fsum[q] + back[q]
    return vals + asum + fsum

def diagonal():
    lanes = lax.broadcasted_iota(jnp.int32, (8, 128), 1)
    return jnp.where(lanes % 8 == lax.broadcasted_iota(jnp.int32, (8, 128), 0), lanes // 8, -1)

def reduced(pending, diag):
    vals, asum, fsum = pending[0:6], pending[6:12], pending[12:18]
    last = [jnp.where(diag == 15, jnp.sum(vals[q], axis=1, keepdims=True), asum[q]) for q in range(6)]
    return [jnp.sum(x, axis=0, keepdims=True) for x in last], [jnp.sum(x, axis=0, keepdims=True) for x in fsum]

def settle(pending, diag, acc, a, b, live):
    asum, fsum = reduced(pending, diag)
    for q in range(6):
        acc[q, pl.ds(a, 1), :] += jnp.where(live, asum[q], 0.0)
    for q in range(6):
        acc[q, pl.ds(b, 1), :] -= jnp.where(live, fsum[q], 0.0)

def greet(bricks):
    me = lax.axis_index("brick")
    barrier = pltpu.get_barrier_semaphore()
    for off in range(1, bricks):
        pl.semaphore_signal(barrier, inc=1, device_id={"brick": lax.rem(me + off, bricks)}, device_id_type=MESH)
    return me, barrier

WAVES = ((0, 0), (1, 7), (2, 6), (3, 5), (4, 4))
NX, NZ = 4, 8

def wave_offsets(wave):
    first, second = WAVES[wave]
    zs = (first,) if first == second else (first, second)
    return [(dx, dz) for dz in zs for dx in range(NX) if (dx, dz) != (0, 0)]

def over_lanes(x, y):
    return lax.dot_general(x.astype(BF16), y.astype(BF16), (((1,), (1,)), ((), ())), preferred_element_type=F32)

LATE = 24

def make_lists(leaves, slots_out, kept, kept_count, lent, plan, lists):
    region = lax.axis_index("region")
    slots, regions, lend = kept.shape[1], plan.shape[0], lent.shape[2]
    lane = lax.broadcasted_iota(jnp.int32, (1, slots), 1)
    live = [lane < kept_count[0]]
    ids = [[kept[0:1, :]], [kept[1:2, :]]]
    step = lax.broadcasted_iota(jnp.int32, (1, lend), 1)
    counts = plan[pl.ds(region, 1), :]
    for j in range(regions):
        live.append(step < jnp.broadcast_to(counts[:, j:j + 1], (1, lend)))
        for side in range(2):
            ids[side].append(lent[j, side:side + 1, :])
    def ones(x):
        return jnp.where(x, 1.0, 0.0)
    live = jnp.concatenate([ones(x) for x in live], axis=1)
    width = live.shape[1]
    first, second = [jnp.concatenate([x.astype(F32) for x in ids[side]], axis=1) for side in range(2)]
    row = lax.broadcasted_iota(jnp.int32, (width, width), 0)
    col = lax.broadcasted_iota(jnp.int32, (width, width), 1)
    def inner(v):
        return jnp.where((v >= leaves) & (lax.rem(v, slots_out) >= slots_out // 2), 0.0, 1.0)
    inside = live * inner(first.astype(jnp.int32)) * inner(second.astype(jnp.int32))
    def before(flags):
        return over_lanes(jnp.broadcast_to(flags, (8, width)), ones(col < row))[0:1]
    late = jnp.where(before(inside) < LATE, inside, 0.0)
    now = live - late
    total = over_lanes(jnp.broadcast_to(now, (8, width)), jnp.ones((width, width), F32))[0:1]
    def moved(values, flags, shift):
        place = jnp.where(flags > 0.0, before(flags) + shift, -1.0).astype(jnp.int32)
        pick = ones(jnp.broadcast_to(place, (width, width)) == row)
        return over_lanes(jnp.broadcast_to(values, (8, width)), pick)[0:1]
    late_a, late_b = moved(first + 1.0, late, 1), moved(second + 1.0, late, 1)
    places = late_a + moved(second + 1.0, late, 1 + width // 2) - 1.0
    out = jnp.concatenate([moved(first, now, 0), moved(second, now, 0), total, jnp.maximum(late_a - 1.0, 0.0),
                           jnp.maximum(late_b - 1.0, 0.0), places, jnp.zeros((2, width), F32)], axis=0)
    lists[...] = out.astype(jnp.int32)

def make_owner(ship, owner):
    leaves, ghosts = owner.shape
    slots, bricks = ship.shape
    leaf = lax.broadcasted_iota(jnp.int32, (leaves, bricks), 0)
    here = [jnp.where(jnp.broadcast_to(ship[k:k + 1, :], (leaves, bricks)) == leaf, 1.0, 0.0) for k in range(slots)]
    ghost = lax.broadcasted_iota(jnp.int32, (ghosts, bricks), 0)
    brick = lax.broadcasted_iota(jnp.int32, (ghosts, bricks), 1)
    total = 0.0
    for k in range(slots):
        total += over_lanes(here[k], jnp.where(ghost == brick * slots + k, 1.0, 0.0))
    owner[...] = total.astype(BF16)

def send_kernel(bricks, slots, seg_hbm, ship_hbm, kept_hbm, count, lent_hbm, plan_hbm,
                feat, left, right, more, lists, owner, axes,
                seg, ship, ship_rows, kept, lent, plan, ext, stage, in_sems, send_sem, recv_sems):
    pairs = ((seg_hbm, seg), (ship_hbm, ship), (ship_hbm, ship_rows), (kept_hbm, kept),
             (lent_hbm, lent), (plan_hbm, plan))
    copies = [pltpu.make_async_copy(src, dst, in_sems.at[i]) for i, (src, dst) in enumerate(pairs)]
    for copy in copies:
        copy.start()
    me, barrier = greet(bricks)
    x, z = me // NZ, lax.rem(me, NZ)
    leaves = seg.shape[0]
    for copy in copies[0:2]:
        copy.wait()
    for q in range(bricks):
        for k in range(slots):
            stage[q * slots + k] = seg[ship[k, q]]
    origin = jnp.broadcast_to(seg[0, 0:3, 0:1], (3, 128))
    def own(i, _):
        for k in range(4):
            j = 4 * i + k
            u, length = prepare(seg[j], origin, feat, left, right, more, j)
            for q in range(3):
                axes[q, pl.ds(j, 1), :] = u[q:q + 1]
            axes[3, pl.ds(j, 1), :] = length
        return 0
    lax.fori_loop(0, leaves // 8, own, 0)
    pl.semaphore_wait(barrier, bricks - 1)
    mine = ext.at[pl.ds(me * slots, slots)]
    for wave in range(len(WAVES)):
        for dx, dz in wave_offsets(wave):
            q = lax.rem(x + dx, NX) * NZ + lax.rem(z + dz, NZ)
            pltpu.make_async_remote_copy(
                src_ref=stage.at[pl.ds(q * slots, slots)], dst_ref=mine, send_sem=send_sem, recv_sem=recv_sems.at[wave],
                device_id={"brick": q}, device_id_type=MESH).start()
    lax.fori_loop(leaves // 8, leaves // 4, own, 0)
    def ghosts(q, source):
        for k in range(slots):
            prepare(source[q * slots + k], origin, feat, left, right, more, leaves + q * slots + k)
    ghosts(me, stage)
    for copy in copies[2:]:
        copy.wait()
    make_lists(leaves, slots, kept, count, lent, plan, lists)
    make_owner(ship_rows, owner)
    for wave in range(len(WAVES)):
        count_in = len(wave_offsets(wave)) * slots
        pltpu.make_async_copy(stage.at[0:count_in], ext.at[0:count_in], recv_sems.at[wave]).wait()
        first, second = WAVES[wave]
        skip = 1 if first == 0 else 0
        def arrived(i, _):
            dz = first + (second - first) * (i // NX)
            q = lax.rem(x + NX - lax.rem(i, NX), NX) * NZ + lax.rem(z + NZ - dz, NZ)
            ghosts(q, ext)
            return 0
        lax.fori_loop(skip, count_in // slots + skip, arrived, 0)
    total = (bricks - 1) * slots
    pltpu.make_async_copy(stage.at[0:total], ext.at[0:total], send_sem).wait()

def back_kernel(bricks, slots, leaves, lists, places, feat, left, right, more, acc, own, back, total, sums,
                spread0, spread1, dots0, dots1, wide0, wide1, pend, send_sem, recv_sems):
    me, barrier = greet(bricks)
    def at(t):
        t = jnp.minimum(t + 1, LATE)
        return lists[3, t], lists[4, t]
    spread0[...] = spread_matrix()
    spread1[...] = spread0[...]
    bufs = ((spread0, dots0, wide0), (spread1, dots1, wide1))
    products(*at(0), left, right, more, *bufs[0])
    pend[...] = jnp.zeros_like(pend)
    sums[...] = jnp.zeros_like(sums)
    diag = diagonal()
    def keep(pending, row):
        asum, fsum = reduced(pending, diag)
        for q in range(6):
            sums[q, pl.ds(row, 1), :] = asum[q]
            sums[q, pl.ds(row + 64, 1), :] = -fsum[q]
    def some(i, _):
        for k in range(LATE_UNROLL):
            t = LATE_UNROLL * i + k
            _, b = at(t)
            products(*at(t + 1), left, right, more, *bufs[(k + 1) % 2])
            if k == 0:
                pending = [pend[q] for q in range(18)]
            keep(pending, t)
            pending = tile(b, feat, *bufs[k % 2][1:], diag)
        for q in range(18):
            pend[q] = pending[q]
        return 0
    half = slots // 2
    def send(half_number, source):
        mine = back.at[:, pl.ds(me * slots + half_number * half, half)]
        for wave in reversed(range(len(WAVES))):
            for dx, dz in wave_offsets(wave):
                q = lax.rem(me // NZ + dx, NX) * NZ + lax.rem(me + dz, NZ)
                pltpu.make_async_remote_copy(
                    src_ref=source.at[:, pl.ds(leaves + q * slots + half_number * half, half)], dst_ref=mine,
                    send_sem=send_sem, recv_sem=recv_sems.at[half_number], device_id={"brick": q}, device_id_type=MESH).start()
    lax.fori_loop(0, EARLY // LATE_UNROLL, some, 0)
    pl.semaphore_wait(barrier, bricks - 1)
    send(1, acc)
    lax.fori_loop(EARLY // LATE_UNROLL, LATE // LATE_UNROLL, some, 0)
    keep([pend[q] for q in range(18)], LATE)
    blocks = total.shape[1]
    pick = jnp.where(lax.broadcasted_iota(jnp.int32, (blocks, 128), 0) == jnp.broadcast_to(places[5:6, :], (blocks, 128)), 1.0, 0.0)
    pick = pick.astype(BF16)
    pick = jnp.concatenate([pick, pick, pick], axis=1)
    for q in range(6):
        parts = jnp.concatenate(split3(sums[q]), axis=0).astype(BF16)
        total[q] = acc[q] + jnp.dot(pick, parts, preferred_element_type=F32)
    send(0, total)
    own[...] = total[:, 0:leaves]
    for q in range(6):
        back[q, pl.ds(me * slots, half)] = total[q, pl.ds(leaves + me * slots, half)]
        back[q, pl.ds(me * slots + half, half)] = acc[q, pl.ds(leaves + me * slots + half, half)]
    sent = (bricks - 1) * half
    for half_number in range(2):
        pltpu.make_async_copy(acc.at[:, 0:sent], back.at[:, 0:sent], recv_sems.at[half_number]).wait()
    pltpu.make_async_copy(acc.at[:, 0:2 * sent], back.at[:, 0:2 * sent], send_sem).wait()

LATE_UNROLL = 4
EARLY = 12
UNROLL = 6

def tile_kernel(lists, feat, left, right, more, acc, spread0, spread1, dots0, dots1, wide0, wide1, pend):
    n = lists[2, 0]
    last = jnp.maximum(n - 1, 0)
    def at(t):
        t = jnp.minimum(jnp.maximum(t, 0), last)
        return lists[0, t], lists[1, t]
    spread0[...] = spread_matrix()
    spread1[...] = spread0[...]
    bufs = ((spread0, dots0, wide0), (spread1, dots1, wide1))
    products(*at(0), left, right, more, *bufs[0])
    acc[...] = jnp.zeros_like(acc)
    pend[...] = jnp.zeros_like(pend)
    diag = diagonal()
    def tiles(first, count):
        for k in range(count):
            t = first + k
            a, b = at(t)
            products(*at(t + 1), left, right, more, *bufs[(k + 1) % 2])
            if k == 0:
                pending = [pend[q] for q in range(18)]
                before = at(t - 1)
                live = True
            settle(pending, diag, acc, *before, live)
            pending = tile(b, feat, *bufs[k % 2][1:], diag)
            before = (a, b)
            live = t < n
        for q in range(18):
            pend[q] = jnp.where(live, pending[q], 0.0)
    def many(i, _):
        tiles(UNROLL * i, UNROLL)
        return 0
    def few(i, _):
        tiles(2 * i, 2)
        return 0
    whole = n // UNROLL
    lax.fori_loop(0, whole, many, 0)
    pairs = (n + 1) // 2
    lax.fori_loop(whole * (UNROLL // 2), pairs, few, 0)
    settle([pend[q] for q in range(18)], diag, acc, *at(2 * pairs - 1), True)

def finish_kernel(axes, owner, own, back, out):
    leaves = out.shape[1]
    pick = owner[...]
    pick = jnp.concatenate([pick, pick, pick], axis=1)
    total = []
    for q in range(6):
        parts = jnp.concatenate(split3(back[q]), axis=0).astype(BF16)
        total.append(own[q] + jnp.dot(pick, parts, preferred_element_type=F32))
    u = [axes[q] for q in range(3)]
    half = 0.5 * axes[3]
    force = total[0:3]
    lever = [total[3 + q] - half * force[q] for q in range(3)]
    for q in range(3):
        out[q] = force[q]
        out[3 + q] = u[(q + 1) % 3] * lever[(q + 2) % 3] - u[(q + 2) % 3] * lever[(q + 1) % 3]

VM = pl.BlockSpec(memory_space=pltpu.VMEM)
SM = pl.BlockSpec(memory_space=pltpu.SMEM)
HB = pl.BlockSpec(memory_space=pltpu.HBM)
LIMIT = 26 * 2**20

def body(segments, ship_list, kept_tiles, kept_count, lent_tiles, lent_count):
    leaves, _, width = segments.shape
    bricks = lax.axis_size("brick")
    slots = ship_list.shape[2]
    ghosts = bricks * slots
    blocks = leaves + ghosts
    def shape(*s, dtype=F32):
        return jax.ShapeDtypeStruct(s, dtype)
    def far(x):
        return pltpu.with_memory_space_constraint(x, pltpu.HBM)
    def room(x):
        return pltpu.VMEM(x.shape, x.dtype)
    ship = jnp.transpose(ship_list[0], (1, 0))
    kept = jnp.transpose(kept_tiles[0], (1, 0))
    lent = jnp.transpose(lent_tiles[0], (0, 2, 1))
    tile_slots = kept_tiles.shape[1] + lent_tiles.shape[1] * lent_tiles.shape[2]
    feat, left, right, more, lists, owner, axes = pl.pallas_call(
        functools.partial(send_kernel, bricks, slots),
        out_shape=(shape(blocks, 8, width), shape(blocks, 128, 128, dtype=BF16), shape(blocks, 48, 384, dtype=BF16),
                   shape(blocks, 16, 768, dtype=BF16), shape(8, tile_slots, dtype=jnp.int32),
                   shape(leaves, ghosts, dtype=BF16), shape(4, leaves, width)),
        in_specs=[HB] * 3 + [SM] + [HB] * 2, out_specs=(VM,) * 7,
        scratch_shapes=[room(segments), pltpu.SMEM(ship.shape, jnp.int32), room(ship), room(kept), room(lent),
                        pltpu.VMEM(lent_count.shape[1:], jnp.int32),
                        pltpu.VMEM((ghosts, 8, width), F32), pltpu.VMEM((ghosts, 8, width), F32),
                        pltpu.SemaphoreType.DMA((6,)), pltpu.SemaphoreType.DMA, pltpu.SemaphoreType.DMA((len(WAVES),))],
        compiler_params=pltpu.CompilerParams(collective_id=0, has_side_effects=True, vmem_limit_bytes=LIMIT),
    )(far(segments), far(ship), far(kept), kept_count, far(lent), far(lent_count[0]))
    buffers = [
        pltpu.VMEM((128, 1280), BF16), pltpu.VMEM((128, 1280), BF16),
        pltpu.VMEM((128, 384), F32), pltpu.VMEM((128, 384), F32),
        pltpu.VMEM((128, 1280), F32), pltpu.VMEM((128, 1280), F32),
        pltpu.VMEM((18, 8, 128), F32),
    ]
    acc = pl.pallas_call(
        tile_kernel,
        out_shape=shape(6, blocks, width),
        in_specs=[SM] + [VM] * 4, out_specs=VM,
        scratch_shapes=buffers,
        compiler_params=pltpu.CompilerParams(vmem_limit_bytes=LIMIT),
    )(lists, feat, left, right, more)
    own, back = pl.pallas_call(
        functools.partial(back_kernel, bricks, slots, leaves),
        out_shape=(shape(6, leaves, width), shape(6, ghosts, width)),
        in_specs=[SM] + [VM] * 6, out_specs=(VM, VM),
        scratch_shapes=[pltpu.VMEM((6, blocks, width), F32), pltpu.VMEM((6, 128, width), F32)] + buffers
        + [pltpu.SemaphoreType.DMA, pltpu.SemaphoreType.DMA((2,))],
        compiler_params=pltpu.CompilerParams(collective_id=1, has_side_effects=True, vmem_limit_bytes=LIMIT),
    )(lists, lists, feat, left, right, more, acc)
    loads = pl.pallas_call(
        finish_kernel,
        out_shape=shape(6, leaves, width),
        in_specs=[VM] * 4, out_specs=VM,
        compiler_params=pltpu.CompilerParams(vmem_limit_bytes=LIMIT),
    )(axes, owner, own, back)
    return jnp.transpose(loads, (1, 0, 2))

def solution(mesh):
    placed = (
        P(("brick", "region"), None, None),
        P(("brick", "region"), None, None),
        P(("brick", "region"), None, None),
        P(("brick", "region")),
        P(("brick", "region"), None, None, None),
        P("brick", None, None),
    )
    return jax.shard_map(body, mesh=mesh, in_specs=placed, out_specs=P(("brick", "region"), None, None), check_vma=False)
```

```python
import functools
import jax, jax.numpy as jnp
from jax import lax
from jax.experimental import pallas as pl
from jax.experimental.pallas import tpu as pltpu
from jax.sharding import PartitionSpec as P

MESH = pl.DeviceIdType.MESH
F32, BF16 = jnp.float32, jnp.bfloat16
DIST_FLOOR = 0.0025
PARALLEL_FLOOR = 0.05
TINY = 1e-20
LARGE = 1e30

def split3(x):
    hi = x.astype(BF16).astype(F32)
    rest = x - hi
    mid = rest.astype(BF16).astype(F32)
    return hi, mid, rest - mid

def prepare(seg, origin, feat, left, right, more, blk):
    p = seg[0:3] - origin
    d = seg[3:6]
    a = jnp.sum(d * d, axis=0, keepdims=True)
    inv = lax.rsqrt(a)
    u = d * inv
    length = a * inv
    along = jnp.sum(u * p, axis=0, keepdims=True)
    r = seg[6:7]
    ir = jnp.minimum(1.0 / r, LARGE)
    ie = jnp.minimum(0.75 / seg[7:8], LARGE)
    one = jnp.ones_like(r)
    x1 = jnp.concatenate([u, p, along, one], axis=0)
    x2 = jnp.concatenate([length, r, ir, ie, jnp.zeros((4, 128), F32)], axis=0)
    feat[blk] = jnp.concatenate([u, length, jnp.zeros((4, 128), F32)], axis=0)
    h1, m1, l1 = split3(x1)
    h2, m2, l2 = split3(x2)
    rows = jnp.concatenate([h1, h1, m1, m1, h1, l1, h2, m2, l2, jnp.ones((8, 128), F32), jnp.zeros((128 - 80, 128), F32)], axis=0)
    left[blk] = rows.astype(BF16).T
    for q, x in enumerate(extra(p, r, ir, ie)):
        more[blk, :, 128 * q:128 * q + 128] = x
    z = jnp.zeros((3, 128), F32)
    z1 = jnp.zeros((1, 128), F32)
    for q, part in enumerate((
        jnp.concatenate([u, z, z1, z1], axis=0),
        jnp.concatenate([-p, z, one, z1], axis=0),
        jnp.concatenate([z, u, z1, -along], axis=0),
    )):
        h, m, l = split3(part)
        right[blk, :, 128 * q:128 * q + 128] = jnp.concatenate([h, m, h, m, l, h], axis=0).astype(BF16)
    return u, length

def extra(p, r, ir, ie):
    row = lax.broadcasted_iota(jnp.int32, (8, 128), 0)
    out = []
    for keep, x in ((-1, -p[0:1]), (-1, -p[1:2]), (-1, -p[2:3]), (1, r), (2, ir), (3, ie)):
        h, m, l = split3(x)
        out.append(jnp.concatenate([jnp.where(row == keep, 1.0, 0.0), h, m, l, jnp.zeros((5, 128), F32)], axis=0).astype(BF16))
    return out

def spread_matrix():
    row = lax.broadcasted_iota(jnp.int32, (128, 128), 0)
    cols = []
    for q in range(6):
        cols.append((row == q) | (row == 16 + q) | (row == 40 + q))
    for q in range(4):
        cols.append((row == 48 + q) | (row == 56 + q) | (row == 64 + q))
    return jnp.concatenate([jnp.where(c, 1.0, 0.0) for c in cols], axis=1).astype(BF16)

def products(a, b, left, right, more, spread, dots, wide):
    lhs = left[a]
    spread[64:80, 384:768] = more[b, :, 0:384]
    spread[64:80, 896:1280] = more[b, :, 384:768]
    dots[...] = jnp.dot(lhs[:, 0:48], right[b], preferred_element_type=F32)
    wide[...] = jnp.dot(lhs[:, 0:80], spread[0:80], preferred_element_type=F32)

def tile(b, feat, dots, wide, diag):
    def lane(q):
        return jnp.broadcast_to(feat[b, q:q + 1, :], (8, 128))
    u2 = [lane(q) for q in range(3)]
    len2 = lane(3)
    fsum = [None] * 6
    asum = [None] * 6
    for g in range(16):
        rs = slice(8 * g, 8 * g + 8)
        w, c, f = [dots[rs, 128 * q:128 * q + 128] for q in range(3)]
        wd = [wide[rs, 128 * q:128 * q + 128] for q in range(10)]
        u1, apart = wd[0:3], wd[3:6]
        len1, reach, ir, ie = wd[6:10]
        den = jnp.maximum(1.0 - w * w, PARALLEL_FLOOR)
        s = (w * f - c) * pltpu.reciprocal(den, approx=True)
        s = jnp.minimum(jnp.maximum(s, 0.0), len1)
        t = jnp.minimum(jnp.maximum(w * s + f, 0.0), len2)
        s = jnp.minimum(jnp.maximum(w * t - c, 0.0), len1)
        gap = [apart[q] + s * u1[q] - t * u2[q] for q in range(3)]
        m = jnp.maximum(gap[0] * gap[0] + gap[1] * gap[1] + gap[2] * gap[2], DIST_FLOOR)
        y = lax.rsqrt(m)
        h = jnp.maximum(reach - m * y, TINY)
        k = (h * h) * (lax.rsqrt(h * ir) * y) * pltpu.reciprocal(ie, approx=True)
        force = [k * x for x in gap]
        vals = force + [s * x for x in force]
        if g < 15:
            for q in range(6):
                red = jnp.sum(vals[q], axis=1, keepdims=True)
                asum[q] = jnp.where(diag == g, red, 0.0 if g == 0 else asum[q])
        back = force + [t * x for x in force]
        for q in range(6):
            fsum[q] = back[q] if g == 0 else fsum[q] + back[q]
    return vals + asum + fsum

def diagonal():
    lanes = lax.broadcasted_iota(jnp.int32, (8, 128), 1)
    return jnp.where(lanes % 8 == lax.broadcasted_iota(jnp.int32, (8, 128), 0), lanes // 8, -1)

def reduced(pending, diag):
    vals, asum, fsum = pending[0:6], pending[6:12], pending[12:18]
    last = [jnp.where(diag == 15, jnp.sum(vals[q], axis=1, keepdims=True), asum[q]) for q in range(6)]
    return [jnp.sum(x, axis=0, keepdims=True) for x in last], [jnp.sum(x, axis=0, keepdims=True) for x in fsum]

def settle(pending, diag, acc, a, b, live):
    asum, fsum = reduced(pending, diag)
    for q in range(6):
        acc[q, pl.ds(a, 1), :] += jnp.where(live, asum[q], 0.0)
    for q in range(6):
        acc[q, pl.ds(b, 1), :] -= jnp.where(live, fsum[q], 0.0)

def greet(bricks):
    me = lax.axis_index("brick")
    barrier = pltpu.get_barrier_semaphore()
    for off in range(1, bricks):
        pl.semaphore_signal(barrier, inc=1, device_id={"brick": lax.rem(me + off, bricks)}, device_id_type=MESH)
    return me, barrier

WAVES = ((0, 0), (1, 7), (2, 6), (3, 5), (4, 4))
NX, NZ = 4, 8

def wave_offsets(wave):
    first, second = WAVES[wave]
    zs = (first,) if first == second else (first, second)
    return [(dx, dz) for dz in zs for dx in range(NX) if (dx, dz) != (0, 0)]

def over_lanes(x, y):
    return lax.dot_general(x.astype(BF16), y.astype(BF16), (((1,), (1,)), ((), ())), preferred_element_type=F32)

LATE = 24

def make_lists(leaves, slots_out, kept, kept_count, lent, plan, lists):
    region = lax.axis_index("region")
    slots, regions, lend = kept.shape[1], plan.shape[0], lent.shape[2]
    lane = lax.broadcasted_iota(jnp.int32, (1, slots), 1)
    live = [lane < kept_count[0]]
    ids = [[kept[0:1, :]], [kept[1:2, :]]]
    step = lax.broadcasted_iota(jnp.int32, (1, lend), 1)
    counts = plan[pl.ds(region, 1), :]
    for j in range(regions):
        live.append(step < jnp.broadcast_to(counts[:, j:j + 1], (1, lend)))
        for side in range(2):
            ids[side].append(lent[j, side:side + 1, :])
    def ones(x):
        return jnp.where(x, 1.0, 0.0)
    live = jnp.concatenate([ones(x) for x in live], axis=1)
    width = live.shape[1]
    first, second = [jnp.concatenate([x.astype(F32) for x in ids[side]], axis=1) for side in range(2)]
    row = lax.broadcasted_iota(jnp.int32, (width, width), 0)
    col = lax.broadcasted_iota(jnp.int32, (width, width), 1)
    def inner(v):
        return jnp.where((v >= leaves) & (lax.rem(v, slots_out) >= slots_out // 2), 0.0, 1.0)
    inside = live * inner(first.astype(jnp.int32)) * inner(second.astype(jnp.int32))
    def before(flags):
        return over_lanes(jnp.broadcast_to(flags, (8, width)), ones(col < row))[0:1]
    late = jnp.where(before(inside) < LATE, inside, 0.0)
    now = live - late
    total = over_lanes(jnp.broadcast_to(now, (8, width)), jnp.ones((width, width), F32))[0:1]
    def moved(values, flags, shift):
        place = jnp.where(flags > 0.0, before(flags) + shift, -1.0).astype(jnp.int32)
        pick = ones(jnp.broadcast_to(place, (width, width)) == row)
        return over_lanes(jnp.broadcast_to(values, (8, width)), pick)[0:1]
    late_a, late_b = moved(first + 1.0, late, 1), moved(second + 1.0, late, 1)
    places = late_a + moved(second + 1.0, late, 1 + width // 2) - 1.0
    out = jnp.concatenate([moved(first, now, 0), moved(second, now, 0), total, jnp.maximum(late_a - 1.0, 0.0),
                           jnp.maximum(late_b - 1.0, 0.0), places, jnp.zeros((2, width), F32)], axis=0)
    lists[...] = out.astype(jnp.int32)

def make_owner(ship, owner):
    leaves, ghosts = owner.shape
    slots, bricks = ship.shape
    leaf = lax.broadcasted_iota(jnp.int32, (leaves, bricks), 0)
    here = [jnp.where(jnp.broadcast_to(ship[k:k + 1, :], (leaves, bricks)) == leaf, 1.0, 0.0) for k in range(slots)]
    ghost = lax.broadcasted_iota(jnp.int32, (ghosts, bricks), 0)
    brick = lax.broadcasted_iota(jnp.int32, (ghosts, bricks), 1)
    total = 0.0
    for k in range(slots):
        total += over_lanes(here[k], jnp.where(ghost == brick * slots + k, 1.0, 0.0))
    owner[...] = total.astype(BF16)

def send_kernel(bricks, slots, seg_hbm, ship_hbm, kept_hbm, count, lent_hbm, plan_hbm,
                feat, left, right, more, lists, owner, axes,
                seg, ship, ship_rows, kept, lent, plan, ext, stage, in_sems, send_sem, recv_sems):
    pairs = ((seg_hbm, seg), (ship_hbm, ship), (ship_hbm, ship_rows), (kept_hbm, kept),
             (lent_hbm, lent), (plan_hbm, plan))
    copies = [pltpu.make_async_copy(src, dst, in_sems.at[i]) for i, (src, dst) in enumerate(pairs)]
    for copy in copies:
        copy.start()
    me, barrier = greet(bricks)
    x, z = me // NZ, lax.rem(me, NZ)
    leaves = seg.shape[0]
    for copy in copies[0:2]:
        copy.wait()
    for q in range(bricks):
        for k in range(slots):
            stage[q * slots + k] = seg[ship[k, q]]
    origin = jnp.broadcast_to(seg[0, 0:3, 0:1], (3, 128))
    def own(i, _):
        for k in range(8):
            j = 8 * i + k
            u, length = prepare(seg[j], origin, feat, left, right, more, j)
            for q in range(3):
                axes[q, pl.ds(j, 1), :] = u[q:q + 1]
            axes[3, pl.ds(j, 1), :] = length
        return 0
    lax.fori_loop(0, leaves // 16, own, 0)
    pl.semaphore_wait(barrier, bricks - 1)
    mine = ext.at[pl.ds(me * slots, slots)]
    for wave in range(len(WAVES)):
        for dx, dz in wave_offsets(wave):
            q = lax.rem(x + dx, NX) * NZ + lax.rem(z + dz, NZ)
            pltpu.make_async_remote_copy(
                src_ref=stage.at[pl.ds(q * slots, slots)], dst_ref=mine, send_sem=send_sem, recv_sem=recv_sems.at[wave],
                device_id={"brick": q}, device_id_type=MESH).start()
    lax.fori_loop(leaves // 16, leaves // 8, own, 0)
    def ghosts(q, source):
        for k in range(slots):
            prepare(source[q * slots + k], origin, feat, left, right, more, leaves + q * slots + k)
    ghosts(me, stage)
    for copy in copies[2:]:
        copy.wait()
    make_lists(leaves, slots, kept, count, lent, plan, lists)
    make_owner(ship_rows, owner)
    for wave in range(len(WAVES)):
        count_in = len(wave_offsets(wave)) * slots
        pltpu.make_async_copy(stage.at[0:count_in], ext.at[0:count_in], recv_sems.at[wave]).wait()
        first, second = WAVES[wave]
        def source(i):
            dz = first + (second - first) * (i // NX)
            return lax.rem(x + NX - lax.rem(i, NX), NX) * NZ + lax.rem(z + NZ - dz, NZ)
        def arrived(i, _):
            ghosts(source(2 * i), ext)
            ghosts(source(2 * i + 1), ext)
            return 0
        if first == 0:
            ghosts(source(1), ext)
        lax.fori_loop(1 if first == 0 else 0, (count_in // slots + 1) // 2, arrived, 0)
    total = (bricks - 1) * slots
    pltpu.make_async_copy(stage.at[0:total], ext.at[0:total], send_sem).wait()

def back_kernel(bricks, slots, leaves, lists, places, feat, left, right, more, acc, own, back, total, sums,
                spread0, spread1, dots0, dots1, wide0, wide1, pend, send_sem, recv_sems):
    me, barrier = greet(bricks)
    def at(t):
        t = jnp.minimum(t + 1, LATE)
        return lists[3, t], lists[4, t]
    spread0[...] = spread_matrix()
    spread1[...] = spread0[...]
    bufs = ((spread0, dots0, wide0), (spread1, dots1, wide1))
    products(*at(0), left, right, more, *bufs[0])
    pend[...] = jnp.zeros_like(pend)
    sums[...] = jnp.zeros_like(sums)
    diag = diagonal()
    def keep(pending, row):
        asum, fsum = reduced(pending, diag)
        for q in range(6):
            sums[q, pl.ds(row, 1), :] = asum[q]
            sums[q, pl.ds(row + 64, 1), :] = -fsum[q]
    def some(i, _):
        for k in range(LATE_UNROLL):
            t = LATE_UNROLL * i + k
            _, b = at(t)
            products(*at(t + 1), left, right, more, *bufs[(k + 1) % 2])
            if k == 0:
                pending = [pend[q] for q in range(18)]
            keep(pending, t)
            pending = tile(b, feat, *bufs[k % 2][1:], diag)
        for q in range(18):
            pend[q] = pending[q]
        return 0
    half = slots // 2
    def send(half_number, source):
        mine = back.at[:, pl.ds(me * slots + half_number * half, half)]
        for wave in reversed(range(len(WAVES))):
            for dx, dz in wave_offsets(wave):
                q = lax.rem(me // NZ + dx, NX) * NZ + lax.rem(me + dz, NZ)
                pltpu.make_async_remote_copy(
                    src_ref=source.at[:, pl.ds(leaves + q * slots + half_number * half, half)], dst_ref=mine,
                    send_sem=send_sem, recv_sem=recv_sems.at[half_number], device_id={"brick": q}, device_id_type=MESH).start()
    lax.fori_loop(0, EARLY // LATE_UNROLL, some, 0)
    pl.semaphore_wait(barrier, bricks - 1)
    send(1, acc)
    lax.fori_loop(EARLY // LATE_UNROLL, LATE // LATE_UNROLL, some, 0)
    keep([pend[q] for q in range(18)], LATE)
    blocks = total.shape[1]
    pick = jnp.where(lax.broadcasted_iota(jnp.int32, (blocks, 128), 0) == jnp.broadcast_to(places[5:6, :], (blocks, 128)), 1.0, 0.0)
    pick = pick.astype(BF16)
    pick = jnp.concatenate([pick, pick, pick], axis=1)
    for q in range(6):
        parts = jnp.concatenate(split3(sums[q]), axis=0).astype(BF16)
        total[q] = acc[q] + jnp.dot(pick, parts, preferred_element_type=F32)
    send(0, total)
    own[...] = total[:, 0:leaves]
    for q in range(6):
        back[q, pl.ds(me * slots, half)] = total[q, pl.ds(leaves + me * slots, half)]
        back[q, pl.ds(me * slots + half, half)] = acc[q, pl.ds(leaves + me * slots + half, half)]
    sent = (bricks - 1) * half
    for half_number in range(2):
        pltpu.make_async_copy(acc.at[:, 0:sent], back.at[:, 0:sent], recv_sems.at[half_number]).wait()
    pltpu.make_async_copy(acc.at[:, 0:2 * sent], back.at[:, 0:2 * sent], send_sem).wait()

LATE_UNROLL = 4
EARLY = 12
UNROLL = 6

def tile_kernel(lists, feat, left, right, more, acc, spread0, spread1, dots0, dots1, wide0, wide1, pend):
    n = lists[2, 0]
    last = jnp.maximum(n - 1, 0)
    def at(t):
        t = jnp.minimum(jnp.maximum(t, 0), last)
        return lists[0, t], lists[1, t]
    spread0[...] = spread_matrix()
    spread1[...] = spread0[...]
    bufs = ((spread0, dots0, wide0), (spread1, dots1, wide1))
    products(*at(0), left, right, more, *bufs[0])
    acc[...] = jnp.zeros_like(acc)
    pend[...] = jnp.zeros_like(pend)
    diag = diagonal()
    def tiles(first, count):
        for k in range(count):
            t = first + k
            a, b = at(t)
            products(*at(t + 1), left, right, more, *bufs[(k + 1) % 2])
            if k == 0:
                pending = [pend[q] for q in range(18)]
                before = at(t - 1)
                live = True
            settle(pending, diag, acc, *before, live)
            pending = tile(b, feat, *bufs[k % 2][1:], diag)
            before = (a, b)
            live = t < n
        for q in range(18):
            pend[q] = jnp.where(live, pending[q], 0.0)
    def many(i, _):
        tiles(UNROLL * i, UNROLL)
        return 0
    def few(i, _):
        tiles(2 * i, 2)
        return 0
    whole = n // UNROLL
    lax.fori_loop(0, whole, many, 0)
    pairs = (n + 1) // 2
    lax.fori_loop(whole * (UNROLL // 2), pairs, few, 0)
    settle([pend[q] for q in range(18)], diag, acc, *at(2 * pairs - 1), True)

def finish_kernel(axes, owner, own, back, out):
    leaves = out.shape[1]
    pick = owner[...]
    pick = jnp.concatenate([pick, pick, pick], axis=1)
    total = []
    for q in range(6):
        parts = jnp.concatenate(split3(back[q]), axis=0).astype(BF16)
        total.append(own[q] + jnp.dot(pick, parts, preferred_element_type=F32))
    u = [axes[q] for q in range(3)]
    half = 0.5 * axes[3]
    force = total[0:3]
    lever = [total[3 + q] - half * force[q] for q in range(3)]
    for q in range(3):
        out[q] = force[q]
        out[3 + q] = u[(q + 1) % 3] * lever[(q + 2) % 3] - u[(q + 2) % 3] * lever[(q + 1) % 3]

VM = pl.BlockSpec(memory_space=pltpu.VMEM)
SM = pl.BlockSpec(memory_space=pltpu.SMEM)
HB = pl.BlockSpec(memory_space=pltpu.HBM)
LIMIT = 26 * 2**20

def body(segments, ship_list, kept_tiles, kept_count, lent_tiles, lent_count):
    leaves, _, width = segments.shape
    bricks = lax.axis_size("brick")
    slots = ship_list.shape[2]
    ghosts = bricks * slots
    blocks = leaves + ghosts
    def shape(*s, dtype=F32):
        return jax.ShapeDtypeStruct(s, dtype)
    def far(x):
        return pltpu.with_memory_space_constraint(x, pltpu.HBM)
    def room(x):
        return pltpu.VMEM(x.shape, x.dtype)
    ship = jnp.transpose(ship_list[0], (1, 0))
    kept = jnp.transpose(kept_tiles[0], (1, 0))
    lent = jnp.transpose(lent_tiles[0], (0, 2, 1))
    tile_slots = kept_tiles.shape[1] + lent_tiles.shape[1] * lent_tiles.shape[2]
    feat, left, right, more, lists, owner, axes = pl.pallas_call(
        functools.partial(send_kernel, bricks, slots),
        out_shape=(shape(blocks, 8, width), shape(blocks, 128, 128, dtype=BF16), shape(blocks, 48, 384, dtype=BF16),
                   shape(blocks, 16, 768, dtype=BF16), shape(8, tile_slots, dtype=jnp.int32),
                   shape(leaves, ghosts, dtype=BF16), shape(4, leaves, width)),
        in_specs=[HB] * 3 + [SM] + [HB] * 2, out_specs=(VM,) * 7,
        scratch_shapes=[room(segments), pltpu.SMEM(ship.shape, jnp.int32), room(ship), room(kept), room(lent),
                        pltpu.VMEM(lent_count.shape[1:], jnp.int32),
                        pltpu.VMEM((ghosts, 8, width), F32), pltpu.VMEM((ghosts, 8, width), F32),
                        pltpu.SemaphoreType.DMA((6,)), pltpu.SemaphoreType.DMA, pltpu.SemaphoreType.DMA((len(WAVES),))],
        compiler_params=pltpu.CompilerParams(collective_id=0, has_side_effects=True, vmem_limit_bytes=LIMIT),
    )(far(segments), far(ship), far(kept), kept_count, far(lent), far(lent_count[0]))
    buffers = [
        pltpu.VMEM((128, 1280), BF16), pltpu.VMEM((128, 1280), BF16),
        pltpu.VMEM((128, 384), F32), pltpu.VMEM((128, 384), F32),
        pltpu.VMEM((128, 1280), F32), pltpu.VMEM((128, 1280), F32),
        pltpu.VMEM((18, 8, 128), F32),
    ]
    acc = pl.pallas_call(
        tile_kernel,
        out_shape=shape(6, blocks, width),
        in_specs=[SM] + [VM] * 4, out_specs=VM,
        scratch_shapes=buffers,
        compiler_params=pltpu.CompilerParams(vmem_limit_bytes=LIMIT),
    )(lists, feat, left, right, more)
    own, back = pl.pallas_call(
        functools.partial(back_kernel, bricks, slots, leaves),
        out_shape=(shape(6, leaves, width), shape(6, ghosts, width)),
        in_specs=[SM] + [VM] * 6, out_specs=(VM, VM),
        scratch_shapes=[pltpu.VMEM((6, blocks, width), F32), pltpu.VMEM((6, 128, width), F32)] + buffers
        + [pltpu.SemaphoreType.DMA, pltpu.SemaphoreType.DMA((2,))],
        compiler_params=pltpu.CompilerParams(collective_id=1, has_side_effects=True, vmem_limit_bytes=LIMIT),
    )(lists, lists, feat, left, right, more, acc)
    loads = pl.pallas_call(
        finish_kernel,
        out_shape=shape(6, leaves, width),
        in_specs=[VM] * 4, out_specs=VM,
        compiler_params=pltpu.CompilerParams(vmem_limit_bytes=LIMIT),
    )(axes, owner, own, back)
    return jnp.transpose(loads, (1, 0, 2))

def solution(mesh):
    placed = (
        P(("brick", "region"), None, None),
        P(("brick", "region"), None, None),
        P(("brick", "region"), None, None),
        P(("brick", "region")),
        P(("brick", "region"), None, None, None),
        P("brick", None, None),
    )
    return jax.shard_map(body, mesh=mesh, in_specs=placed, out_specs=P(("brick", "region"), None, None), check_vma=False)
```
